512 devices in a mesh: dp: 8 (over z), fsdp: 8 (over x, core), tensor: 8 (over y).
Axes of the slice: x: 4, y: 8, z: 8, core: 2. Of those that a mesh axis runs over, the one named last changes fastest.
Arguments:
- momentum: float32 [8, 1, 7168, 2048], P('dp', None, 'fsdp', 'tensor'), may hold values from -500 to 500
- gradient: bfloat16 [8, 1, 7168, 2048], P('dp', None, 'fsdp', 'tensor'), may hold values from -3 to 3
- right_factor: float32 [1, 2048, 128], P(None, 'tensor'), may hold values from -0.125 to 0.125
Outputs:
- new_momentum: float32 [8, 1, 7168, 2048], P('dp', None, 'fsdp', 'tensor')
- right_out: float32 [1, 2048, 128], P(None, 'tensor')
- update: bfloat16 [1, 7168, 2048], P(None, 'fsdp', 'tensor')
The draws below stay inside these ranges and needn't reach their ends.
All inputs are finite; a program needn't handle non-finite values.
Results may differ from the reference program's by a relative error of at most 0.001.
Values sent between devices are 32-bit elements; how exact they have to be, the bound alone decides.
No kernel may reach another device: no remote copies, remote signals or barrier semaphores. Data moves between devices by JAX's collectives and lax.ppermute only.
A program may use at most 64 MiB of HBM per device.

```python
import math
import jax
import jax.numpy as jnp
from jax import lax

M_ROWS = 7168
N_COLS = 2048
RANK = 128
EXPERTS = 1
REPLICAS = 8
N_DP = 8


def draw_momentum(key, part):
    key = jax.random.fold_in(key, 11)
    key_rows, key_cols, key_own = jax.random.split(key, 3)
    spread = 10.0
    ramp_rows = jnp.arange(M_ROWS, dtype=jnp.float32) / M_ROWS - 0.5
    ramp_cols = jnp.arange(N_COLS, dtype=jnp.float32) / N_COLS - 0.5
    row_scale = jnp.exp(jax.random.uniform(key_rows, (EXPERTS, M_ROWS, 1), jnp.float32, -0.5, 0.5) * math.log(spread) + math.log(3.0) * ramp_rows[None, :, None])
    col_scale = jnp.exp(jax.random.uniform(key_cols, (EXPERTS, 1, N_COLS), jnp.float32, -0.5, 0.5) * math.log(spread) + math.log(3.0) * ramp_cols[None, None, :])
    own = jnp.clip(jax.random.normal(key_own, (REPLICAS, EXPERTS, M_ROWS, N_COLS), jnp.float32), -6.0, 6.0)
    field = own
    return (field * row_scale[None] * col_scale[None]).astype(jnp.float32)


def block_levels(key, dims, pieces, low, high):
    def one(position, parts):
        draws = jax.random.uniform(jax.random.fold_in(jax.random.fold_in(key, 6), position), (parts,), jnp.float32, low / len(pieces), high / len(pieces))
        return jnp.repeat(jnp.exp(draws), dims[position] // parts).reshape((-1,) + (1,) * (len(dims) - position - 1))

    level = one(*pieces[0])
    for cut in pieces[1:]:
        level = level * one(*cut)
    return level


def noise(stream_key, extent, deviation, reach, shards=(), held_as=jnp.bfloat16):
    entries = deviation * jax.random.normal(stream_key, extent, jnp.float32)
    if shards:
        entries = entries * block_levels(stream_key, extent, shards, -0.22, 0.18)
    return jnp.clip(entries, -reach, reach).astype(held_as)


def setup_inputs(seed: int = 0) -> dict:
    streams_of = jax.random.split(jax.random.key(seed), 4)
    return {
        "momentum": draw_momentum(jax.random.fold_in(streams_of[3], 71), 0),
        "gradient": noise(streams_of[1], (REPLICAS, EXPERTS, M_ROWS, N_COLS), 0.5, 3.0, ((0, 8), (2, 8), (3, 8))),
        "right_factor": noise(streams_of[2], (EXPERTS, N_COLS, RANK), N_COLS ** -0.5, 0.125, ((1, 8),), jnp.float32),
    }


def reference(momentum, gradient, right_factor):
    highest = lax.Precision.HIGHEST
    moments = []
    rights = []
    updates = []
    for expert in range(EXPERTS):
        blended = momentum[:, expert] + gradient[:, expert].astype(jnp.float32)
        right_prev = right_factor[expert]
        projected = jnp.einsum('dmn,nr->mr', blended, right_prev, precision=highest)
        gram_matrix = jnp.dot(projected.T.astype(jnp.float32), projected.astype(jnp.float32), precision=highest, preferred_element_type=jnp.float32)
        factor_low = jnp.linalg.cholesky(gram_matrix)
        orthonormal = jax.scipy.linalg.solve_triangular(factor_low, projected.T, lower=True).T
        reduced = jnp.einsum('dmn,mr->nr', blended, orthonormal, precision=highest) / N_DP
        squares = lax.optimization_barrier(jnp.sum(reduced * reduced, axis=0))
        right_new = reduced / (jnp.sqrt(squares) + 1e-06)
        outer = jnp.dot(orthonormal.astype(jnp.float32), reduced.T.astype(jnp.float32), precision=highest, preferred_element_type=jnp.float32)
        moments.append(blended - (1.0 - 0.95) * outer[None])
        rights.append(right_new)
        direction = jnp.dot(orthonormal.astype(jnp.float32), right_new.T.astype(jnp.float32), precision=highest, preferred_element_type=jnp.float32)
        updates.append((math.sqrt(M_ROWS * N_COLS / RANK) * direction).astype(jnp.bfloat16))
    return (jnp.stack(moments, axis=1), jnp.stack(rights), jnp.stack(updates))
```

```python
import math

import jax
import jax.numpy as jnp
from jax import lax
from jax.sharding import PartitionSpec as P

M_ROWS = 7168
N_COLS = 2048
RANK = 128


highest = lax.Precision.HIGHEST
decay_rate = 0.95
epsilon = 1e-06


def product(left, right):
    return jnp.dot(left, right, precision=highest, preferred_element_type=jnp.float32)


def inner_rows(left, right):
    return lax.dot_general(
        left, right, (((0,), (0,)), ((), ())), precision=highest, preferred_element_type=jnp.float32
    )


def outer_cols(left, right):
    return lax.dot_general(
        left, right, (((1,), (1,)), ((), ())), precision=highest, preferred_element_type=jnp.float32
    )


def whiten(matrix, factor_low):
    return jax.scipy.linalg.solve_triangular(factor_low, matrix.T, lower=True).T


def scatter_sum(blocks, axes):
    return jnp.sum(lax.all_to_all(blocks, axes, 0, 0), axis=0)


def gather(block, axes, count):
    return lax.all_to_all(jnp.broadcast_to(block, (count,) + block.shape), axes, 0, 0)


def body(momentum, gradient, right_factor):
    n_dp, n_fsdp, n_tensor = (lax.axis_size(a) for a in ("dp", "fsdp", "tensor"))
    blended = momentum[0, 0] + gradient[0, 0].astype(jnp.float32)
    rows, cols = blended.shape
    plane = n_dp * n_tensor
    partial = product(blended, right_factor[0])
    part = scatter_sum(partial.reshape(plane, rows // plane, RANK), ("dp", "tensor"))
    projected = gather(part, ("dp", "tensor"), plane).reshape(rows, RANK)
    right_raw = inner_rows(blended, projected).reshape(n_fsdp, cols // n_fsdp, RANK)
    gram = inner_rows(projected, projected).reshape(n_fsdp, RANK // n_fsdp, RANK)
    held = scatter_sum(jnp.concatenate([right_raw, gram], axis=1), "fsdp")
    own = cols // n_fsdp
    summed = jnp.sum(gather(held[:own], "dp", n_dp), axis=0)
    whole = gather(jnp.concatenate([summed, held[own:]], axis=0), "fsdp", n_fsdp)
    right_raw = whole[:, :own].reshape(cols, RANK)
    factor_low = jnp.linalg.cholesky(whole[:, own:].reshape(RANK, RANK))
    both = whiten(jnp.concatenate([projected, right_raw / n_dp], axis=0), factor_low)
    projected, reduced = both[:rows], both[rows:]
    squares = jnp.sum(reduced * reduced, axis=0, keepdims=True)
    squares = jnp.sum(gather(squares, "tensor", n_tensor), axis=0)
    right_new = reduced / (jnp.sqrt(squares) + epsilon)
    moment = blended - (1.0 - decay_rate) * outer_cols(projected, reduced)
    direction = outer_cols(projected, right_new)
    update = (math.sqrt(M_ROWS * N_COLS / RANK) * direction).astype(jnp.bfloat16)
    return moment[None, None], right_new[None], update[None]


def solution(mesh):
    in_specs = (
        P("dp", None, "fsdp", "tensor"),
        P("dp", None, "fsdp", "tensor"),
        P(None, "tensor", None),
    )
    out_specs = (
        P("dp", None, "fsdp", "tensor"),
        P(None, "tensor", None),
        P(None, "fsdp", "tensor"),
    )
    return jax.shard_map(body, mesh=mesh, in_specs=in_specs, out_specs=out_specs, check_vma=False)
```

```python
import math

import jax
import jax.numpy as jnp
from jax import lax
from jax.experimental import pallas as pl
from jax.experimental.pallas import tpu as pltpu
from jax.sharding import PartitionSpec as P

M_ROWS = 7168
N_COLS = 2048
RANK = 128
SUB = 8


highest = lax.Precision.HIGHEST
decay_rate = 0.95
epsilon = 1e-06


def product(left, right):
    return jnp.dot(left, right, precision=highest, preferred_element_type=jnp.float32)


def inner_rows(left, right):
    return lax.dot_general(
        left, right, (((0,), (0,)), ((), ())), precision=highest, preferred_element_type=jnp.float32
    )


def outer_cols(left, right):
    return lax.dot_general(
        left, right, (((1,), (1,)), ((), ())), precision=highest, preferred_element_type=jnp.float32
    )


def spread(row, count=SUB):
    return jnp.broadcast_to(row, (count, RANK))

def invert_factor(tiles, write):
    lane = lax.broadcasted_iota(jnp.int32, (SUB, RANK), 1)
    count = len(tiles)
    for b in range(count):
        first = b * SUB
        panel = (lane >= first) & (lane < first + SUB)
        below = range(b, count)
        columns = {t: [jnp.broadcast_to(tiles[t][:, first + k:first + k + 1], (SUB, RANK)) for k in range(SUB)] for t in below}
        pivot = [[spread(columns[b][j][k:k + 1]) if k >= j else None for k in range(SUB)] for j in range(SUB)]
        rows = [jnp.where(panel, (lane == first + p).astype(jnp.float32), spread(tiles[b][p:p + 1])) for p in range(SUB)]
        inverse = []
        ratio = {}
        for j in range(SUB):
            inverse.append(1.0 / pivot[j][j])
            for i in range(j + 1, SUB):
                ratio[i, j] = pivot[j][i] * inverse[j]
                for k in range(i, SUB):
                    pivot[i][k] = pivot[i][k] - ratio[i, j] * pivot[j][k]
                rows[i] = rows[i] - ratio[i, j] * rows[j]
        for t in range(b + 1, count):
            held = jnp.where(panel, 0.0, tiles[t])
            left = columns[t]
            for j in range(SUB):
                multiple = left[j] * inverse[j]
                for k in range(j + 1, SUB):
                    left[k] = left[k] - multiple * pivot[j][k]
                held = held - multiple * rows[j]
            tiles[t] = held
        for p in range(SUB):
            d = pivot[p][p]
            root = lax.rsqrt(d)
            root = root * (1.5 - 0.5 * d * root * root)
            write(first + p, jnp.where(lane <= first + p, rows[p] * root, 0.0)[0:1])

def factor_kernel(parts_ref, out_ref):
    tiles = [jnp.sum(parts_ref[:, t * SUB:(t + 1) * SUB, :], axis=0) for t in range(RANK // SUB)]

    def write(row, value):
        out_ref[row:row + 1, :] = value

    invert_factor(tiles, write)


def inverse_of_factor(parts):
    count = parts.shape[0]
    return pl.pallas_call(
        factor_kernel,
        grid=(1,),
        out_shape=jax.ShapeDtypeStruct((RANK, RANK), jnp.float32),
        in_specs=[pl.BlockSpec((count, RANK, RANK), lambda i: (0, 0, 0))],
        out_specs=pl.BlockSpec((RANK, RANK), lambda i: (0, 0)),
        compiler_params=pltpu.CompilerParams(vmem_limit_bytes=16 * 2**20),
        cost_estimate=pl.CostEstimate(flops=4_000_000, bytes_accessed=4 * (count + 1) * RANK**2, transcendentals=0),
    )(parts)


def scatter_sum(blocks, axes):
    return jnp.sum(lax.all_to_all(blocks, axes, 0, 0), axis=0)


def gather(block, axes, count):
    return lax.all_to_all(jnp.broadcast_to(block, (count,) + block.shape), axes, 0, 0)


def body(momentum, gradient, right_factor):
    n_dp, n_fsdp, n_tensor = (lax.axis_size(a) for a in ("dp", "fsdp", "tensor"))
    blended = momentum[0, 0] + gradient[0, 0].astype(jnp.float32)
    rows, cols = blended.shape
    plane = n_dp * n_tensor
    partial = product(blended, right_factor[0])
    part = scatter_sum(partial.reshape(plane, rows // plane, RANK), ("dp", "tensor"))
    projected = gather(part, ("dp", "tensor"), plane).reshape(rows, RANK)
    own = cols // n_fsdp
    right_raw = inner_rows(blended, projected).reshape(n_fsdp, own, RANK)
    gram = inner_rows(projected, projected)
    sent = jnp.concatenate([jnp.broadcast_to(gram, (n_fsdp, RANK, RANK)), right_raw], axis=1)
    parts = lax.all_to_all(sent, "fsdp", 0, 0)
    replicas = gather(jnp.sum(parts[:, RANK:], axis=0), "dp", n_dp)
    inverse_low = inverse_of_factor(parts)
    reduced_own = outer_cols(jnp.sum(replicas, axis=0), inverse_low) / n_dp
    reduced = gather(reduced_own, "fsdp", n_fsdp).reshape(cols, RANK)
    squares = gather(jnp.sum(reduced_own * reduced_own, axis=0, keepdims=True), ("fsdp", "tensor"), n_fsdp * n_tensor)
    orthonormal = outer_cols(projected, inverse_low)
    moment = blended - (1.0 - decay_rate) * outer_cols(orthonormal, reduced)
    right_new = reduced / (jnp.sqrt(jnp.sum(squares, axis=0)) + epsilon)
    direction = outer_cols(orthonormal, right_new)
    update = (math.sqrt(M_ROWS * N_COLS / RANK) * direction).astype(jnp.bfloat16)
    return moment[None, None], right_new[None], update[None]


def solution(mesh):
    in_specs = (
        P("dp", None, "fsdp", "tensor"),
        P("dp", None, "fsdp", "tensor"),
        P(None, "tensor", None),
    )
    out_specs = (
        P("dp", None, "fsdp", "tensor"),
        P(None, "tensor", None),
        P(None, "fsdp", "tensor"),
    )
    return jax.shard_map(body, mesh=mesh, in_specs=in_specs, out_specs=out_specs, check_vma=False)
```

```python
import math

import jax
import jax.numpy as jnp
from jax import lax
from jax.experimental import pallas as pl
from jax.experimental.pallas import tpu as pltpu
from jax.sharding import PartitionSpec as P

M_ROWS = 7168
N_COLS = 2048
RANK = 128
SUB = 8


highest = lax.Precision.HIGHEST
decay_rate = 0.95
epsilon = 1e-06


def product(left, right):
    return jnp.dot(left, right, precision=highest, preferred_element_type=jnp.float32)


def inner_rows(left, right):
    return lax.dot_general(
        left, right, (((0,), (0,)), ((), ())), precision=highest, preferred_element_type=jnp.float32
    )


def outer_cols(left, right):
    return lax.dot_general(
        left, right, (((1,), (1,)), ((), ())), precision=highest, preferred_element_type=jnp.float32
    )


def spread(row, count=SUB):
    return jnp.broadcast_to(row, (count, RANK))

def invert_factor(tiles, write):
    lane = lax.broadcasted_iota(jnp.int32, (SUB, RANK), 1)
    count = len(tiles)
    for b in range(count):
        first = b * SUB
        panel = (lane >= first) & (lane < first + SUB)
        below = range(b, count)
        columns = {t: [jnp.broadcast_to(tiles[t][:, first + k:first + k + 1], (SUB, RANK)) for k in range(SUB)] for t in below}
        pivot = [[spread(columns[b][j][k:k + 1]) if k >= j else None for k in range(SUB)] for j in range(SUB)]
        rows = [jnp.where(panel, (lane == first + p).astype(jnp.float32), spread(tiles[b][p:p + 1])) for p in range(SUB)]
        inverse = []
        ratio = {}
        for j in range(SUB):
            inverse.append(1.0 / pivot[j][j])
            for i in range(j + 1, SUB):
                ratio[i, j] = pivot[j][i] * inverse[j]
                for k in range(i, SUB):
                    pivot[i][k] = pivot[i][k] - ratio[i, j] * pivot[j][k]
                rows[i] = rows[i] - ratio[i, j] * rows[j]
        for t in range(b + 1, count):
            held = jnp.where(panel, 0.0, tiles[t])
            left = columns[t]
            for j in range(SUB):
                multiple = left[j] * inverse[j]
                for k in range(j + 1, SUB):
                    left[k] = left[k] - multiple * pivot[j][k]
                held = held - multiple * rows[j]
            tiles[t] = held
        for p in range(SUB):
            d = pivot[p][p]
            root = lax.rsqrt(d)
            root = root * (1.5 - 0.5 * d * root * root)
            write(first + p, jnp.where(lane <= first + p, rows[p] * root, 0.0)[0:1])

def factor_kernel(upper_ref, lower_ref, out_ref):
    half = RANK // 2
    tiles = [ref[t:t + SUB, :] for ref in (upper_ref, lower_ref) for t in range(0, half, SUB)]

    def write(row, value):
        out_ref[row:row + 1, :] = value

    invert_factor(tiles, write)


def inverse_of_factor(upper, lower):
    return pl.pallas_call(
        factor_kernel,
        out_shape=jax.ShapeDtypeStruct((RANK, RANK), jnp.float32),
        in_specs=[pl.BlockSpec(memory_space=pltpu.VMEM)] * 2,
        out_specs=pl.BlockSpec(memory_space=pltpu.VMEM),
        compiler_params=pltpu.CompilerParams(vmem_limit_bytes=16 * 2**20),
        cost_estimate=pl.CostEstimate(flops=4_000_000, bytes_accessed=8 * RANK**2, transcendentals=0),
    )(upper, lower)


def inner_kernel(blended_ref, projected_ref, out_ref):
    count, high, _ = out_ref.shape
    half = RANK // 2
    own = high - half
    projected = projected_ref[...]
    flipped = projected.T
    right_raw = product(flipped, blended_ref[...]).T
    gram = product(flipped, projected)
    for k in range(count):
        out_ref[k, :own] = right_raw[k * own:(k + 1) * own]
        out_ref[k, own:] = gram[k % 2 * half:(k % 2 + 1) * half]


def inner_products(blended, projected, count):
    rows, cols = blended.shape
    high = cols // count + RANK // 2
    return pl.pallas_call(
        inner_kernel,
        out_shape=jax.ShapeDtypeStruct((count, high, RANK), jnp.float32),
        in_specs=[pl.BlockSpec(memory_space=pltpu.VMEM)] * 2,
        out_specs=pl.BlockSpec(memory_space=pltpu.VMEM),
        compiler_params=pltpu.CompilerParams(vmem_limit_bytes=24 * 2**20),
        cost_estimate=pl.CostEstimate(
            flops=2 * rows * (cols + RANK) * RANK, bytes_accessed=4 * rows * (cols + RANK), transcendentals=0
        ),
    )(blended, projected)


def scatter_sum(blocks, axes):
    return jnp.sum(lax.all_to_all(blocks, axes, 0, 0), axis=0)


def gather(block, axes, count):
    return lax.all_to_all(jnp.broadcast_to(block, (count,) + block.shape), axes, 0, 0)


def body(momentum, gradient, right_factor):
    n_dp, n_fsdp, n_tensor = (lax.axis_size(a) for a in ("dp", "fsdp", "tensor"))
    blended = momentum[0, 0] + gradient[0, 0].astype(jnp.float32)
    rows, cols = blended.shape
    plane = n_dp * n_tensor
    partial = product(blended, right_factor[0])
    part = scatter_sum(partial.reshape(plane, rows // plane, RANK), ("dp", "tensor"))
    projected = gather(part, ("dp", "tensor"), plane).reshape(rows, RANK)
    own = cols // n_fsdp
    parts = scatter_sum(inner_products(blended, projected, n_fsdp), "fsdp")
    replicas = gather(parts[:own], "dp", n_dp)
    mine = parts[own:]
    other = lax.ppermute(mine, "fsdp", [(k, k ^ 1) for k in range(n_fsdp)])
    even = lax.axis_index("fsdp") % 2 == 0
    inverse_low = inverse_of_factor(jnp.where(even, mine, other), jnp.where(even, other, mine))
    orthonormal = outer_cols(projected, inverse_low)
    replicas, orthonormal = lax.optimization_barrier((replicas, orthonormal))
    reduced_own = outer_cols(jnp.sum(replicas, axis=0), inverse_low) / n_dp
    reduced = gather(reduced_own, "fsdp", n_fsdp).reshape(cols, RANK)
    squares = gather(jnp.sum(reduced * reduced, axis=0, keepdims=True), "tensor", n_tensor)
    moment = blended - (1.0 - decay_rate) * outer_cols(orthonormal, reduced)
    right_new = reduced / (jnp.sqrt(jnp.sum(squares, axis=0)) + epsilon)
    direction = outer_cols(orthonormal, right_new)
    update = (math.sqrt(M_ROWS * N_COLS / RANK) * direction).astype(jnp.bfloat16)
    return moment[None, None], right_new[None], update[None]


def solution(mesh):
    in_specs = (
        P("dp", None, "fsdp", "tensor"),
        P("dp", None, "fsdp", "tensor"),
        P(None, "tensor", None),
    )
    out_specs = (
        P("dp", None, "fsdp", "tensor"),
        P(None, "tensor", None),
        P(None, "fsdp", "tensor"),
    )
    return jax.shard_map(body, mesh=mesh, in_specs=in_specs, out_specs=out_specs, check_vma=False)
```

```python
import math

import jax
import jax.numpy as jnp
from jax import lax
from jax.experimental import pallas as pl
from jax.experimental.pallas import tpu as pltpu
from jax.sharding import PartitionSpec as P

M_ROWS = 7168
N_COLS = 2048
RANK = 128
SUB = 8
REPLICAS = 8


highest = lax.Precision.HIGHEST
decay_rate = 0.95
epsilon = 1e-06


def product(left, right):
    return jnp.dot(left, right, precision=highest, preferred_element_type=jnp.float32)


def inner_rows(left, right):
    return lax.dot_general(
        left, right, (((0,), (0,)), ((), ())), precision=highest, preferred_element_type=jnp.float32
    )


def outer_cols(left, right):
    return lax.dot_general(
        left, right, (((1,), (1,)), ((), ())), precision=highest, preferred_element_type=jnp.float32
    )


def spread(row, count=SUB):
    return jnp.broadcast_to(row, (count, RANK))

def invert_factor(tiles, write):
    lane = lax.broadcasted_iota(jnp.int32, (SUB, RANK), 1)
    count = len(tiles)
    for b in range(count):
        first = b * SUB
        panel = (lane >= first) & (lane < first + SUB)
        below = range(b, count)
        columns = {t: [jnp.broadcast_to(tiles[t][:, first + k:first + k + 1], (SUB, RANK)) for k in range(SUB)] for t in below}
        pivot = [[spread(columns[b][j][k:k + 1]) if k >= j else None for k in range(SUB)] for j in range(SUB)]
        rows = [jnp.where(panel, (lane == first + p).astype(jnp.float32), spread(tiles[b][p:p + 1])) for p in range(SUB)]
        inverse = []
        ratio = {}
        for j in range(SUB):
            inverse.append(1.0 / pivot[j][j])
            for i in range(j + 1, SUB):
                ratio[i, j] = pivot[j][i] * inverse[j]
                for k in range(i, SUB):
                    pivot[i][k] = pivot[i][k] - ratio[i, j] * pivot[j][k]
                rows[i] = rows[i] - ratio[i, j] * rows[j]
        for t in range(b + 1, count):
            held = jnp.where(panel, 0.0, tiles[t])
            left = columns[t]
            for j in range(SUB):
                multiple = left[j] * inverse[j]
                for k in range(j + 1, SUB):
                    left[k] = left[k] - multiple * pivot[j][k]
                held = held - multiple * rows[j]
            tiles[t] = held
        for p in range(SUB):
            d = pivot[p][p]
            root = lax.rsqrt(d)
            root = root * (1.5 - 0.5 * d * root * root)
            write(first + p, jnp.where(lane <= first + p, rows[p] * root, 0.0)[0:1])

def whiten_kernel(whole_ref, inverse_ref, reduced_ref, squares_ref):
    count, high, _ = whole_ref.shape
    share = RANK // count
    own = high - share
    tiles = [whole_ref[k, t:t + SUB] for k in range(count) for t in range(own, high, SUB)]

    def write(row, value):
        inverse_ref[row:row + 1, :] = value

    invert_factor(tiles, write)
    right_raw = jnp.concatenate([whole_ref[k, :own] for k in range(count)], axis=0)
    reduced = outer_cols(right_raw, inverse_ref[...]) * (1.0 / REPLICAS)
    reduced_ref[...] = reduced
    squares = jnp.sum(reduced * reduced, axis=0, keepdims=True)
    for k in range(squares_ref.shape[0]):
        squares_ref[k] = squares


def whiten_right(whole, n_tensor):
    count, high, _ = whole.shape
    cols = count * high - RANK
    vmem = pl.BlockSpec(memory_space=pltpu.VMEM)
    return pl.pallas_call(
        whiten_kernel,
        out_shape=(
            jax.ShapeDtypeStruct((RANK, RANK), jnp.float32),
            jax.ShapeDtypeStruct((cols, RANK), jnp.float32),
            jax.ShapeDtypeStruct((n_tensor, 1, RANK), jnp.float32),
        ),
        in_specs=[vmem],
        out_specs=[vmem] * 3,
        compiler_params=pltpu.CompilerParams(vmem_limit_bytes=16 * 2**20),
    )(whole)


def inner_kernel(blended_ref, projected_ref, out_ref):
    count, high, _ = out_ref.shape
    share = RANK // count
    own = high - share
    projected = projected_ref[...]
    flipped = projected.T
    right_raw = product(flipped, blended_ref[...]).T
    gram = product(flipped, projected)
    for k in range(count):
        out_ref[k, :own] = right_raw[k * own:(k + 1) * own]
        out_ref[k, own:] = gram[k * share:(k + 1) * share]


def inner_products(blended, projected, count):
    rows, cols = blended.shape
    vmem = pl.BlockSpec(memory_space=pltpu.VMEM)
    return pl.pallas_call(
        inner_kernel,
        out_shape=jax.ShapeDtypeStruct((count, (cols + RANK) // count, RANK), jnp.float32),
        in_specs=[vmem] * 2,
        out_specs=vmem,
        compiler_params=pltpu.CompilerParams(vmem_limit_bytes=24 * 2**20),
    )(blended, projected)


def halves(x):
    high = x.astype(jnp.bfloat16)
    return high, (x - high.astype(jnp.float32)).astype(jnp.bfloat16)


def update_kernel(left_ref, reduced_ref, squares_ref, right_out, update_out, right_ref, update_ref, sems):
    steps = sems.shape[0] - 1
    rows = left_ref.shape[0] // steps

    def outer(left, right):
        return lax.dot_general(left, right, (((1,), (1,)), ((), ())), preferred_element_type=jnp.float32)

    norm = jnp.sqrt(jnp.sum(squares_ref[...], axis=0)) + epsilon
    right_new = reduced_ref[...] / norm
    right_ref[...] = right_new
    copies = [pltpu.make_async_copy(right_ref, right_out, sems.at[steps])]
    copies[0].start()
    right_high, right_low = halves(right_new * math.sqrt(M_ROWS * N_COLS / RANK))
    for step in range(steps):
        block = pl.ds(step * rows, rows)
        left_high, left_low = halves(left_ref[block, :])
        total = outer(left_high, right_high) + (outer(left_high, right_low) + outer(left_low, right_high))
        update_ref[block, :] = total.astype(jnp.bfloat16)
        copies.append(pltpu.make_async_copy(update_ref.at[block], update_out.at[block], sems.at[step]))
        copies[-1].start()
    for copy in copies:
        copy.wait()


def update_and_right(left, reduced, squares):
    steps = 4
    rows, cols = left.shape[0], reduced.shape[0]
    vmem, anywhere = pl.BlockSpec(memory_space=pltpu.VMEM), pl.BlockSpec(memory_space=pl.ANY)
    return pl.pallas_call(
        update_kernel,
        out_shape=(
            jax.ShapeDtypeStruct((cols, RANK), jnp.float32),
            jax.ShapeDtypeStruct((rows, cols), jnp.bfloat16),
        ),
        in_specs=[vmem] * 3,
        out_specs=[anywhere] * 2,
        scratch_shapes=[
            pltpu.VMEM((cols, RANK), jnp.float32),
            pltpu.VMEM((rows, cols), jnp.bfloat16),
            pltpu.SemaphoreType.DMA((steps + 1,)),
        ],
        compiler_params=pltpu.CompilerParams(vmem_limit_bytes=16 * 2**20),
    )(left, reduced, squares)


def scatter_sum(blocks, axes):
    return jnp.sum(lax.all_to_all(blocks, axes, 0, 0), axis=0)


def gather(block, axes, count):
    return lax.all_to_all(jnp.broadcast_to(block, (count,) + block.shape), axes, 0, 0)


def body(momentum, gradient, right_factor):
    n_dp, n_fsdp, n_tensor = (lax.axis_size(a) for a in ("dp", "fsdp", "tensor"))
    blended = momentum[0, 0] + gradient[0, 0].astype(jnp.float32)
    rows, cols = blended.shape
    plane = n_dp * n_tensor
    partial = lax.optimization_barrier(product(blended, right_factor[0]))
    part = scatter_sum(partial.reshape(plane, rows // plane, RANK), ("dp", "tensor"))
    projected = gather(part, ("dp", "tensor"), plane).reshape(rows, RANK)
    own = cols // n_fsdp
    held = scatter_sum(inner_products(blended, projected, n_fsdp), "fsdp")
    summed = jnp.sum(gather(held[:own], "dp", n_dp), axis=0)
    whole = gather(jnp.concatenate([summed, held[own:]], axis=0), "fsdp", n_fsdp)
    inverse_low, reduced, squares = whiten_right(whole, n_tensor)
    squares = lax.all_to_all(squares, "tensor", 0, 0)
    orthonormal = outer_cols(projected, inverse_low)
    moment = blended - (1.0 - decay_rate) * outer_cols(orthonormal, reduced)
    right_new, update = update_and_right(orthonormal, reduced, squares)
    return moment[None, None], right_new[None], update[None]


def solution(mesh):
    in_specs = (
        P("dp", None, "fsdp", "tensor"),
        P("dp", None, "fsdp", "tensor"),
        P(None, "tensor", None),
    )
    out_specs = (
        P("dp", None, "fsdp", "tensor"),
        P(None, "tensor", None),
        P(None, "fsdp", "tensor"),
    )
    return jax.shard_map(body, mesh=mesh, in_specs=in_specs, out_specs=out_specs, check_vma=False)
```

```python
import math

import jax
import jax.numpy as jnp
from jax import lax
from jax.experimental import pallas as pl
from jax.experimental.pallas import tpu as pltpu
from jax.sharding import PartitionSpec as P

M_ROWS = 7168
N_COLS = 2048
RANK = 128
SUB = 8
REPLICAS = 8


highest = lax.Precision.HIGHEST
decay_rate = 0.95
epsilon = 1e-06


def product(left, right):
    return jnp.dot(left, right, precision=highest, preferred_element_type=jnp.float32)


def inner_rows(left, right):
    return lax.dot_general(
        left, right, (((0,), (0,)), ((), ())), precision=highest, preferred_element_type=jnp.float32
    )


def outer_cols(left, right):
    return lax.dot_general(
        left, right, (((1,), (1,)), ((), ())), precision=highest, preferred_element_type=jnp.float32
    )


def spread(row, count=SUB):
    return jnp.broadcast_to(row, (count, RANK))

def invert_factor(tiles, write):
    lane = lax.broadcasted_iota(jnp.int32, (SUB, RANK), 1)
    count = len(tiles)
    for b in range(count):
        first = b * SUB
        panel = (lane >= first) & (lane < first + SUB)
        below = range(b, count)
        columns = {t: [jnp.broadcast_to(tiles[t][:, first + k:first + k + 1], (SUB, RANK)) for k in range(SUB)] for t in below}
        pivot = [[spread(columns[b][j][k:k + 1]) if k >= j else None for k in range(SUB)] for j in range(SUB)]
        rows = [jnp.where(panel, (lane == first + p).astype(jnp.float32), spread(tiles[b][p:p + 1])) for p in range(SUB)]
        inverse = []
        ratio = {}
        for j in range(SUB):
            inverse.append(1.0 / pivot[j][j])
            for i in range(j + 1, SUB):
                ratio[i, j] = pivot[j][i] * inverse[j]
                for k in range(i, SUB):
                    pivot[i][k] = pivot[i][k] - ratio[i, j] * pivot[j][k]
                rows[i] = rows[i] - ratio[i, j] * rows[j]
        for t in range(b + 1, count):
            held = jnp.where(panel, 0.0, tiles[t])
            left = columns[t]
            for j in range(SUB):
                multiple = left[j] * inverse[j]
                for k in range(j + 1, SUB):
                    left[k] = left[k] - multiple * pivot[j][k]
                held = held - multiple * rows[j]
            tiles[t] = held
        for p in range(SUB):
            d = pivot[p][p]
            root = lax.rsqrt(d)
            root = root * (1.5 - 0.5 * d * root * root)
            write(first + p, jnp.where(lane <= first + p, rows[p] * root, 0.0)[0:1])

def whiten_kernel(whole_ref, inverse_ref, reduced_ref, squares_ref):
    count, high, _ = whole_ref.shape
    share = RANK // count
    own = high - share
    tiles = [whole_ref[k, t:t + SUB] for k in range(count) for t in range(own, high, SUB)]

    def write(row, value):
        inverse_ref[row:row + 1, :] = value

    invert_factor(tiles, write)
    right_raw = jnp.concatenate([whole_ref[k, :own] for k in range(count)], axis=0)
    reduced = outer_cols(right_raw, inverse_ref[...]) * (1.0 / REPLICAS)
    reduced_ref[...] = reduced
    squares = jnp.sum(reduced * reduced, axis=0, keepdims=True)
    for k in range(squares_ref.shape[0]):
        squares_ref[k] = squares


def whiten_right(whole, n_tensor):
    count, high, _ = whole.shape
    cols = count * high - RANK
    vmem = pl.BlockSpec(memory_space=pltpu.VMEM)
    return pl.pallas_call(
        whiten_kernel,
        out_shape=(
            jax.ShapeDtypeStruct((RANK, RANK), jnp.float32),
            jax.ShapeDtypeStruct((cols, RANK), jnp.float32),
            jax.ShapeDtypeStruct((n_tensor, 1, RANK), jnp.float32),
        ),
        in_specs=[vmem],
        out_specs=[vmem] * 3,
        compiler_params=pltpu.CompilerParams(vmem_limit_bytes=16 * 2**20),
    )(whole)


def inner_kernel(blended_ref, projected_ref, out_ref):
    count, high, _ = out_ref.shape
    share = RANK // count
    own = high - share
    projected = projected_ref[...]
    flipped = projected.T
    right_raw = product(flipped, blended_ref[...]).T
    gram = product(flipped, projected)
    for k in range(count):
        out_ref[k, :own] = right_raw[k * own:(k + 1) * own]
        out_ref[k, own:] = gram[k * share:(k + 1) * share]


def inner_products(blended, projected, count):
    rows, cols = blended.shape
    vmem = pl.BlockSpec(memory_space=pltpu.VMEM)
    return pl.pallas_call(
        inner_kernel,
        out_shape=jax.ShapeDtypeStruct((count, (cols + RANK) // count, RANK), jnp.float32),
        in_specs=[vmem] * 2,
        out_specs=vmem,
        compiler_params=pltpu.CompilerParams(vmem_limit_bytes=24 * 2**20),
    )(blended, projected)


def halves(x):
    high = x.astype(jnp.bfloat16)
    return high, (x - high.astype(jnp.float32)).astype(jnp.bfloat16)


def outer_of_halves(left, right):
    def outer(left, right):
        return lax.dot_general(left, right, (((1,), (1,)), ((), ())), preferred_element_type=jnp.float32)

    return outer(left[0], right[0]) + (outer(left[0], right[1]) + outer(left[1], right[0]))


def moment_kernel(blended_ref, projected_ref, inverse_ref, reduced_ref, left_ref, moment_out, moment_ref, sems):
    steps = sems.shape[0]
    rows = left_ref.shape[0] // steps
    inverse = inverse_ref[...]
    right = halves(reduced_ref[...] * (1.0 - decay_rate))
    copies = []
    for step in range(steps):
        block = pl.ds(step * rows, rows)
        left = outer_cols(projected_ref[block, :], inverse)
        left_ref[block, :] = left
        moment_ref[block, :] = blended_ref[block, :] - outer_of_halves(halves(left), right)
        copies.append(pltpu.make_async_copy(moment_ref.at[block], moment_out.at[block], sems.at[step]))
        copies[-1].start()
    for copy in copies:
        copy.wait()


def left_and_moment(blended, projected, inverse_low, reduced):
    steps = 4
    rows, cols = blended.shape
    vmem, anywhere = pl.BlockSpec(memory_space=pltpu.VMEM), pl.BlockSpec(memory_space=pl.ANY)
    return pl.pallas_call(
        moment_kernel,
        out_shape=(
            jax.ShapeDtypeStruct((rows, RANK), jnp.float32),
            jax.ShapeDtypeStruct((rows, cols), jnp.float32),
        ),
        in_specs=[vmem] * 4,
        out_specs=[vmem, anywhere],
        scratch_shapes=[pltpu.VMEM((rows, cols), jnp.float32), pltpu.SemaphoreType.DMA((steps,))],
        compiler_params=pltpu.CompilerParams(vmem_limit_bytes=24 * 2**20),
        cost_estimate=pl.CostEstimate(
            flops=12 * rows * cols * RANK, bytes_accessed=4 * rows * cols, transcendentals=0
        ),
    )(blended, projected, inverse_low, reduced)


def update_kernel(left_ref, reduced_ref, squares_ref, right_out, update_out, right_ref, update_ref, sems):
    steps = sems.shape[0] - 1
    rows = left_ref.shape[0] // steps

    norm = jnp.sqrt(jnp.sum(squares_ref[...], axis=0)) + epsilon
    right_new = reduced_ref[...] / norm
    right_ref[...] = right_new
    copies = [pltpu.make_async_copy(right_ref, right_out, sems.at[steps])]
    copies[0].start()
    right = halves(right_new * math.sqrt(M_ROWS * N_COLS / RANK))
    for step in range(steps):
        block = pl.ds(step * rows, rows)
        update_ref[block, :] = outer_of_halves(halves(left_ref[block, :]), right).astype(jnp.bfloat16)
        copies.append(pltpu.make_async_copy(update_ref.at[block], update_out.at[block], sems.at[step]))
        copies[-1].start()
    for copy in copies:
        copy.wait()


def update_and_right(left, reduced, squares):
    steps = 4
    rows, cols = left.shape[0], reduced.shape[0]
    vmem, anywhere = pl.BlockSpec(memory_space=pltpu.VMEM), pl.BlockSpec(memory_space=pl.ANY)
    return pl.pallas_call(
        update_kernel,
        out_shape=(
            jax.ShapeDtypeStruct((cols, RANK), jnp.float32),
            jax.ShapeDtypeStruct((rows, cols), jnp.bfloat16),
        ),
        in_specs=[vmem] * 3,
        out_specs=[anywhere] * 2,
        scratch_shapes=[
            pltpu.VMEM((cols, RANK), jnp.float32),
            pltpu.VMEM((rows, cols), jnp.bfloat16),
            pltpu.SemaphoreType.DMA((steps + 1,)),
        ],
        compiler_params=pltpu.CompilerParams(vmem_limit_bytes=16 * 2**20),
    )(left, reduced, squares)


def scatter_sum(blocks, axes):
    return jnp.sum(lax.all_to_all(blocks, axes, 0, 0), axis=0)


def gather(block, axes, count):
    return lax.all_to_all(jnp.broadcast_to(block, (count,) + block.shape), axes, 0, 0)


def split_at(rows, where):
    return rows[:where], rows[where:]


def body(momentum, gradient, right_factor):
    n_dp, n_fsdp, n_tensor = (lax.axis_size(a) for a in ("dp", "fsdp", "tensor"))
    blended = momentum[0, 0] + gradient[0, 0].astype(jnp.float32)
    rows, cols = blended.shape
    plane = n_dp * n_tensor
    partial = lax.optimization_barrier(product(blended, right_factor[0]))
    part = scatter_sum(partial.reshape(plane, rows // plane, RANK), ("tensor", "dp"))
    projected = gather(part, ("tensor", "dp"), plane).reshape(rows, RANK)
    own = cols // n_fsdp
    right_raw, gram = lax.optimization_barrier(
        split_at(scatter_sum(inner_products(blended, projected, n_fsdp), "fsdp"), own)
    )
    summed, gram = lax.optimization_barrier((jnp.sum(gather(right_raw, "dp", n_dp), axis=0), gram))
    whole = gather(jnp.concatenate([summed, gram], axis=0), "fsdp", n_fsdp)
    inverse_low, reduced, squares = whiten_right(whole, n_tensor)
    squares = lax.all_to_all(squares, "tensor", 0, 0)
    orthonormal, moment = left_and_moment(blended, projected, inverse_low, reduced)
    right_new, update = update_and_right(orthonormal, reduced, squares)
    return moment[None, None], right_new[None], update[None]


def solution(mesh):
    in_specs = (
        P("dp", None, "fsdp", "tensor"),
        P("dp", None, "fsdp", "tensor"),
        P(None, "tensor", None),
    )
    out_specs = (
        P("dp", None, "fsdp", "tensor"),
        P(None, "tensor", None),
        P(None, "fsdp", "tensor"),
    )
    return jax.shard_map(body, mesh=mesh, in_specs=in_specs, out_specs=out_specs, check_vma=False)
```

```python
import math

import jax
import jax.numpy as jnp
from jax import lax
from jax.experimental import pallas as pl
from jax.experimental.pallas import tpu as pltpu
from jax.sharding import PartitionSpec as P

M_ROWS = 7168
N_COLS = 2048
RANK = 128
SUB = 8
REPLICAS = 8


highest = lax.Precision.HIGHEST
decay_rate = 0.95
epsilon = 1e-06


def product(left, right):
    return jnp.dot(left, right, precision=highest, preferred_element_type=jnp.float32)


def inner_rows(left, right):
    return lax.dot_general(
        left, right, (((0,), (0,)), ((), ())), precision=highest, preferred_element_type=jnp.float32
    )


def outer_cols(left, right):
    return lax.dot_general(
        left, right, (((1,), (1,)), ((), ())), precision=highest, preferred_element_type=jnp.float32
    )


def spread(row, count=SUB):
    return jnp.broadcast_to(row, (count, RANK))

def invert_factor(tiles, write):
    lane = lax.broadcasted_iota(jnp.int32, (SUB, RANK), 1)
    count = len(tiles)
    for b in range(count):
        first = b * SUB
        panel = (lane >= first) & (lane < first + SUB)
        below = range(b, count)
        columns = {t: [jnp.broadcast_to(tiles[t][:, first + k:first + k + 1], (SUB, RANK)) for k in range(SUB)] for t in below}
        pivot = [[spread(columns[b][j][k:k + 1]) if k >= j else None for k in range(SUB)] for j in range(SUB)]
        rows = [jnp.where(panel, (lane == first + p).astype(jnp.float32), spread(tiles[b][p:p + 1])) for p in range(SUB)]
        inverse = []
        ratio = {}
        for j in range(SUB):
            inverse.append(1.0 / pivot[j][j])
            for i in range(j + 1, SUB):
                ratio[i, j] = pivot[j][i] * inverse[j]
                for k in range(i, SUB):
                    pivot[i][k] = pivot[i][k] - ratio[i, j] * pivot[j][k]
                rows[i] = rows[i] - ratio[i, j] * rows[j]
        for t in range(b + 1, count):
            held = jnp.where(panel, 0.0, tiles[t])
            left = columns[t]
            for j in range(SUB):
                multiple = left[j] * inverse[j]
                for k in range(j + 1, SUB):
                    left[k] = left[k] - multiple * pivot[j][k]
                held = held - multiple * rows[j]
            tiles[t] = held
        for p in range(SUB):
            d = pivot[p][p]
            root = lax.rsqrt(d)
            root = root * (1.5 - 0.5 * d * root * root)
            write(first + p, jnp.where(lane <= first + p, rows[p] * root, 0.0)[0:1])

def whiten_kernel(whole_ref, inverse_ref, reduced_ref, squares_ref):
    count, high, _ = whole_ref.shape
    share = RANK // count
    own = high - share
    tiles = [whole_ref[k, t:t + SUB] for k in range(count) for t in range(own, high, SUB)]

    def write(row, value):
        inverse_ref[row:row + 1, :] = value

    invert_factor(tiles, write)
    right_raw = jnp.concatenate([whole_ref[k, :own] for k in range(count)], axis=0)
    reduced = outer_cols(right_raw, inverse_ref[...]) * (1.0 / REPLICAS)
    reduced_ref[...] = reduced
    squares = jnp.sum(reduced * reduced, axis=0, keepdims=True)
    for k in range(squares_ref.shape[0]):
        squares_ref[k] = squares


def whiten_right(whole, n_tensor):
    count, high, _ = whole.shape
    cols = count * high - RANK
    vmem = pl.BlockSpec(memory_space=pltpu.VMEM)
    return pl.pallas_call(
        whiten_kernel,
        out_shape=(
            jax.ShapeDtypeStruct((RANK, RANK), jnp.float32),
            jax.ShapeDtypeStruct((cols, RANK), jnp.float32),
            jax.ShapeDtypeStruct((n_tensor, 1, RANK), jnp.float32),
        ),
        in_specs=[vmem],
        out_specs=[vmem] * 3,
        compiler_params=pltpu.CompilerParams(vmem_limit_bytes=16 * 2**20),
    )(whole)


def inner_kernel(blended_ref, projected_ref, out_ref):
    count, high, _ = out_ref.shape
    share = RANK // count
    own = high - share
    projected = projected_ref[...]
    flipped = projected.T
    right_raw = product(flipped, blended_ref[...]).T
    gram = product(flipped, projected)
    for k in range(count):
        out_ref[k, :own] = right_raw[k * own:(k + 1) * own]
        out_ref[k, own:] = gram[k * share:(k + 1) * share]


def inner_products(blended, projected, count):
    rows, cols = blended.shape
    vmem = pl.BlockSpec(memory_space=pltpu.VMEM)
    return pl.pallas_call(
        inner_kernel,
        out_shape=jax.ShapeDtypeStruct((count, (cols + RANK) // count, RANK), jnp.float32),
        in_specs=[vmem] * 2,
        out_specs=vmem,
        compiler_params=pltpu.CompilerParams(vmem_limit_bytes=24 * 2**20),
    )(blended, projected)


def halves(x):
    high = x.astype(jnp.bfloat16)
    return high, (x - high.astype(jnp.float32)).astype(jnp.bfloat16)


def outer_of_halves(left, right):
    def outer(left, right):
        return lax.dot_general(left, right, (((1,), (1,)), ((), ())), preferred_element_type=jnp.float32)

    return outer(left[0], right[0]) + (outer(left[0], right[1]) + outer(left[1], right[0]))


def moment_kernel(blended_ref, projected_ref, inverse_ref, reduced_ref, left_ref, moment_out, moment_ref, sems):
    steps = sems.shape[0]
    rows = left_ref.shape[0] // steps
    inverse = inverse_ref[...]
    right = halves(reduced_ref[...] * (1.0 - decay_rate))
    copies = []
    for step in range(steps):
        block = pl.ds(step * rows, rows)
        left = outer_cols(projected_ref[block, :], inverse)
        left_ref[block, :] = left
        moment_ref[block, :] = blended_ref[block, :] - outer_of_halves(halves(left), right)
        copies.append(pltpu.make_async_copy(moment_ref.at[block], moment_out.at[block], sems.at[step]))
        copies[-1].start()
    for copy in copies:
        copy.wait()


def left_and_moment(blended, projected, inverse_low, reduced):
    steps = 4
    rows, cols = blended.shape
    vmem, anywhere = pl.BlockSpec(memory_space=pltpu.VMEM), pl.BlockSpec(memory_space=pl.ANY)
    return pl.pallas_call(
        moment_kernel,
        out_shape=(
            jax.ShapeDtypeStruct((rows, RANK), jnp.float32),
            jax.ShapeDtypeStruct((rows, cols), jnp.float32),
        ),
        in_specs=[vmem] * 4,
        out_specs=[vmem, anywhere],
        scratch_shapes=[pltpu.VMEM((rows, cols), jnp.float32), pltpu.SemaphoreType.DMA((steps,))],
        compiler_params=pltpu.CompilerParams(vmem_limit_bytes=24 * 2**20),
        cost_estimate=pl.CostEstimate(
            flops=12 * rows * cols * RANK, bytes_accessed=4 * rows * cols, transcendentals=0
        ),
    )(blended, projected, inverse_low, reduced)


def update_kernel(left_ref, reduced_ref, squares_ref, right_out, update_out, right_ref, update_ref, sems):
    steps = sems.shape[0] - 1
    rows = left_ref.shape[0] // steps

    norm = jnp.sqrt(jnp.sum(squares_ref[...], axis=0)) + epsilon
    right_new = reduced_ref[...] / norm
    right_ref[...] = right_new
    copies = [pltpu.make_async_copy(right_ref, right_out, sems.at[steps])]
    copies[0].start()
    right = halves(right_new * math.sqrt(M_ROWS * N_COLS / RANK))
    for step in range(steps):
        block = pl.ds(step * rows, rows)
        update_ref[block, :] = outer_of_halves(halves(left_ref[block, :]), right).astype(jnp.bfloat16)
        copies.append(pltpu.make_async_copy(update_ref.at[block], update_out.at[block], sems.at[step]))
        copies[-1].start()
    for copy in copies:
        copy.wait()


def update_and_right(left, reduced, squares):
    steps = 4
    rows, cols = left.shape[0], reduced.shape[0]
    vmem, anywhere = pl.BlockSpec(memory_space=pltpu.VMEM), pl.BlockSpec(memory_space=pl.ANY)
    return pl.pallas_call(
        update_kernel,
        out_shape=(
            jax.ShapeDtypeStruct((cols, RANK), jnp.float32),
            jax.ShapeDtypeStruct((rows, cols), jnp.bfloat16),
        ),
        in_specs=[vmem] * 3,
        out_specs=[anywhere] * 2,
        scratch_shapes=[
            pltpu.VMEM((cols, RANK), jnp.float32),
            pltpu.VMEM((rows, cols), jnp.bfloat16),
            pltpu.SemaphoreType.DMA((steps + 1,)),
        ],
        compiler_params=pltpu.CompilerParams(vmem_limit_bytes=16 * 2**20),
    )(left, reduced, squares)


def scatter_sum(blocks, axes):
    return jnp.sum(lax.all_to_all(blocks, axes, 0, 0), axis=0)


def gather(block, axes, count):
    return lax.all_to_all(jnp.broadcast_to(block, (count,) + block.shape), axes, 0, 0)


def body(momentum, gradient, right_factor):
    n_far, n_near, n_fsdp, n_tensor = (lax.axis_size(a) for a in ("dp_far", "dp_near", "fsdp", "tensor"))
    blended = momentum[0, 0] + gradient[0, 0].astype(jnp.float32)
    rows, cols = blended.shape
    plane = ("dp_far", "dp_near", "tensor")
    count = n_far * n_near * n_tensor
    blocks, lines = (count, rows // count, RANK), (count, 1, rows // count * RANK)
    partial = lax.optimization_barrier(product(blended, right_factor[0]))
    parts = lax.all_to_all(partial.reshape(lines), plane, 0, 0).reshape(rows, RANK)
    part = jnp.sum(lax.optimization_barrier(parts).reshape(blocks), axis=0)
    copies = lax.optimization_barrier(jnp.broadcast_to(part, blocks).reshape(rows, RANK))
    projected = lax.all_to_all(copies.reshape(lines), plane, 0, 0).reshape(rows, RANK)
    group = ("fsdp", "dp_near")
    count = n_fsdp * n_near
    own = cols // count
    held = scatter_sum(inner_products(blended, projected, count), group)
    right_raw, gram = lax.optimization_barrier((held[:own], held[own:] * (1.0 / n_near)))
    summed, gram = lax.optimization_barrier((jnp.sum(gather(right_raw, "dp_far", n_far), axis=0), gram))
    whole = gather(jnp.concatenate([summed, gram], axis=0), group, count)
    inverse_low, reduced, squares = whiten_right(whole, n_tensor)
    squares = lax.all_to_all(squares, "tensor", 0, 0)
    orthonormal, moment = left_and_moment(blended, projected, inverse_low, reduced)
    right_new, update = update_and_right(orthonormal, reduced, squares)
    return moment[None, None], right_new[None], update[None]


def solution(mesh):
    near = 2
    n_dp, n_fsdp, n_tensor = (mesh.shape[a] for a in ("dp", "fsdp", "tensor"))
    devices = mesh.devices.reshape(n_dp // near, near, n_fsdp, n_tensor)
    mesh = jax.sharding.Mesh(devices, ("dp_far", "dp_near", "fsdp", "tensor"))
    dp = ("dp_far", "dp_near")
    in_specs = (
        P(dp, None, "fsdp", "tensor"),
        P(dp, None, "fsdp", "tensor"),
        P(None, "tensor", None),
    )
    out_specs = (
        P(dp, None, "fsdp", "tensor"),
        P(None, "tensor", None),
        P(None, "fsdp", "tensor"),
    )
    return jax.shard_map(body, mesh=mesh, in_specs=in_specs, out_specs=out_specs, check_vma=False)
```

```python
import math

import jax
import jax.numpy as jnp
from jax import lax
from jax.experimental import pallas as pl
from jax.experimental.pallas import tpu as pltpu
from jax.sharding import PartitionSpec as P

M_ROWS = 7168
N_COLS = 2048
RANK = 128
SUB = 8
REPLICAS = 8
DP = ("dp_4", "dp_2", "dp_1")


highest = lax.Precision.HIGHEST
decay_rate = 0.95
epsilon = 1e-06


def product(left, right):
    return jnp.dot(left, right, precision=highest, preferred_element_type=jnp.float32)


def inner_rows(left, right):
    return lax.dot_general(
        left, right, (((0,), (0,)), ((), ())), precision=highest, preferred_element_type=jnp.float32
    )


def outer_cols(left, right):
    return lax.dot_general(
        left, right, (((1,), (1,)), ((), ())), precision=highest, preferred_element_type=jnp.float32
    )


def spread(row, count=SUB):
    return jnp.broadcast_to(row, (count, RANK))

def invert_factor(tiles, write):
    lane = lax.broadcasted_iota(jnp.int32, (SUB, RANK), 1)
    count = len(tiles)
    for b in range(count):
        first = b * SUB
        panel = (lane >= first) & (lane < first + SUB)
        below = range(b, count)
        columns = {t: [jnp.broadcast_to(tiles[t][:, first + k:first + k + 1], (SUB, RANK)) for k in range(SUB)] for t in below}
        pivot = [[spread(columns[b][j][k:k + 1]) if k >= j else None for k in range(SUB)] for j in range(SUB)]
        rows = [jnp.where(panel, (lane == first + p).astype(jnp.float32), spread(tiles[b][p:p + 1])) for p in range(SUB)]
        inverse = []
        ratio = {}
        for j in range(SUB):
            inverse.append(1.0 / pivot[j][j])
            for i in range(j + 1, SUB):
                ratio[i, j] = pivot[j][i] * inverse[j]
                for k in range(i, SUB):
                    pivot[i][k] = pivot[i][k] - ratio[i, j] * pivot[j][k]
                rows[i] = rows[i] - ratio[i, j] * rows[j]
        for t in range(b + 1, count):
            held = jnp.where(panel, 0.0, tiles[t])
            left = columns[t]
            for j in range(SUB):
                multiple = left[j] * inverse[j]
                for k in range(j + 1, SUB):
                    left[k] = left[k] - multiple * pivot[j][k]
                held = held - multiple * rows[j]
            tiles[t] = held
        for p in range(SUB):
            d = pivot[p][p]
            root = lax.rsqrt(d)
            root = root * (1.5 - 0.5 * d * root * root)
            write(first + p, jnp.where(lane <= first + p, rows[p] * root, 0.0)[0:1])

def whiten_kernel(whole_ref, inverse_ref, reduced_ref, squares_ref):
    count, high, _ = whole_ref.shape
    share = RANK // count
    own = high - share
    tiles = [whole_ref[k, t:t + SUB] for k in range(count) for t in range(own, high, SUB)]

    def write(row, value):
        inverse_ref[row:row + 1, :] = value

    invert_factor(tiles, write)
    right_raw = jnp.concatenate([whole_ref[k, :own] for k in range(count)], axis=0)
    reduced = outer_cols(right_raw, inverse_ref[...]) * (1.0 / REPLICAS)
    reduced_ref[...] = reduced
    squares = jnp.sum(reduced * reduced, axis=0, keepdims=True)
    for k in range(squares_ref.shape[0]):
        squares_ref[k] = squares


def whiten_right(whole, n_tensor):
    count, high, _ = whole.shape
    cols = count * high - RANK
    vmem = pl.BlockSpec(memory_space=pltpu.VMEM)
    return pl.pallas_call(
        whiten_kernel,
        out_shape=(
            jax.ShapeDtypeStruct((RANK, RANK), jnp.float32),
            jax.ShapeDtypeStruct((cols, RANK), jnp.float32),
            jax.ShapeDtypeStruct((n_tensor, 1, RANK), jnp.float32),
        ),
        in_specs=[vmem],
        out_specs=[vmem] * 3,
        compiler_params=pltpu.CompilerParams(vmem_limit_bytes=16 * 2**20),
    )(whole)


def inner_kernel(blended_ref, projected_ref, out_ref):
    count, high, _ = out_ref.shape
    share = RANK // count
    own = high - share
    projected = projected_ref[...]
    flipped = projected.T
    right_raw = product(flipped, blended_ref[...]).T
    gram = product(flipped, projected)
    for k in range(count):
        out_ref[k, :own] = right_raw[k * own:(k + 1) * own]
        out_ref[k, own:] = gram[k * share:(k + 1) * share]


def inner_products(blended, projected, count):
    rows, cols = blended.shape
    vmem = pl.BlockSpec(memory_space=pltpu.VMEM)
    return pl.pallas_call(
        inner_kernel,
        out_shape=jax.ShapeDtypeStruct((count, (cols + RANK) // count, RANK), jnp.float32),
        in_specs=[vmem] * 2,
        out_specs=vmem,
        compiler_params=pltpu.CompilerParams(vmem_limit_bytes=24 * 2**20),
    )(blended, projected)


def halves(x):
    high = x.astype(jnp.bfloat16)
    return high, (x - high.astype(jnp.float32)).astype(jnp.bfloat16)


def outer_of_halves(left, right):
    def outer(left, right):
        return lax.dot_general(left, right, (((1,), (1,)), ((), ())), preferred_element_type=jnp.float32)

    return outer(left[0], right[0]) + (outer(left[0], right[1]) + outer(left[1], right[0]))


def moment_kernel(blended_ref, projected_ref, inverse_ref, reduced_ref, left_ref, moment_out, moment_ref, sems):
    steps = sems.shape[0]
    rows = left_ref.shape[0] // steps
    inverse = inverse_ref[...]
    right = halves(reduced_ref[...] * (1.0 - decay_rate))
    copies = []
    for step in range(steps):
        block = pl.ds(step * rows, rows)
        left = outer_cols(projected_ref[block, :], inverse)
        left_ref[block, :] = left
        moment_ref[block, :] = blended_ref[block, :] - outer_of_halves(halves(left), right)
        copies.append(pltpu.make_async_copy(moment_ref.at[block], moment_out.at[block], sems.at[step]))
        copies[-1].start()
    for copy in copies:
        copy.wait()


def left_and_moment(blended, projected, inverse_low, reduced):
    steps = 4
    rows, cols = blended.shape
    vmem, anywhere = pl.BlockSpec(memory_space=pltpu.VMEM), pl.BlockSpec(memory_space=pl.ANY)
    return pl.pallas_call(
        moment_kernel,
        out_shape=(
            jax.ShapeDtypeStruct((rows, RANK), jnp.float32),
            jax.ShapeDtypeStruct((rows, cols), jnp.float32),
        ),
        in_specs=[vmem] * 4,
        out_specs=[vmem, anywhere],
        scratch_shapes=[pltpu.VMEM((rows, cols), jnp.float32), pltpu.SemaphoreType.DMA((steps,))],
        compiler_params=pltpu.CompilerParams(vmem_limit_bytes=24 * 2**20),
        cost_estimate=pl.CostEstimate(
            flops=12 * rows * cols * RANK, bytes_accessed=4 * rows * cols, transcendentals=0
        ),
    )(blended, projected, inverse_low, reduced)


def update_kernel(left_ref, reduced_ref, squares_ref, right_out, update_out, right_ref, update_ref, sems):
    steps = sems.shape[0] - 1
    rows = left_ref.shape[0] // steps

    norm = jnp.sqrt(jnp.sum(squares_ref[...], axis=0)) + epsilon
    right_new = reduced_ref[...] / norm
    right_ref[...] = right_new
    copies = [pltpu.make_async_copy(right_ref, right_out, sems.at[steps])]
    copies[0].start()
    right = halves(right_new * math.sqrt(M_ROWS * N_COLS / RANK))
    for step in range(steps):
        block = pl.ds(step * rows, rows)
        update_ref[block, :] = outer_of_halves(halves(left_ref[block, :]), right).astype(jnp.bfloat16)
        copies.append(pltpu.make_async_copy(update_ref.at[block], update_out.at[block], sems.at[step]))
        copies[-1].start()
    for copy in copies:
        copy.wait()


def update_and_right(left, reduced, squares):
    steps = 4
    rows, cols = left.shape[0], reduced.shape[0]
    vmem, anywhere = pl.BlockSpec(memory_space=pltpu.VMEM), pl.BlockSpec(memory_space=pl.ANY)
    return pl.pallas_call(
        update_kernel,
        out_shape=(
            jax.ShapeDtypeStruct((cols, RANK), jnp.float32),
            jax.ShapeDtypeStruct((rows, cols), jnp.bfloat16),
        ),
        in_specs=[vmem] * 3,
        out_specs=[anywhere] * 2,
        scratch_shapes=[
            pltpu.VMEM((cols, RANK), jnp.float32),
            pltpu.VMEM((rows, cols), jnp.bfloat16),
            pltpu.SemaphoreType.DMA((steps + 1,)),
        ],
        compiler_params=pltpu.CompilerParams(vmem_limit_bytes=16 * 2**20),
    )(left, reduced, squares)


def scatter_sum(blocks, axes):
    return jnp.sum(lax.all_to_all(blocks, axes, 0, 0), axis=0)


def gather(block, axes, count):
    return lax.all_to_all(jnp.broadcast_to(block, (count,) + block.shape), axes, 0, 0)


def body(momentum, gradient, right_factor):
    n_dp, n_near, n_fsdp, n_tensor = (lax.axis_size(a) for a in (DP, "dp_1", "fsdp", "tensor"))
    blended = momentum[0, 0] + gradient[0, 0].astype(jnp.float32)
    rows, cols = blended.shape
    plane = ("tensor", "dp_1", "dp_2", "dp_4")
    count = n_dp * n_tensor
    blocks, lines = (count, rows // count, RANK), (count, 1, rows // count * RANK)
    partial = lax.optimization_barrier(product(blended, right_factor[0]))
    parts = lax.all_to_all(partial.reshape(lines), plane, 0, 0).reshape(rows, RANK)
    part = jnp.sum(lax.optimization_barrier(parts).reshape(blocks), axis=0)
    copies = lax.optimization_barrier(jnp.broadcast_to(part, blocks).reshape(rows, RANK))
    projected = lax.all_to_all(copies.reshape(lines), plane, 0, 0).reshape(rows, RANK)
    group, far = ("dp_1", "fsdp"), ("dp_2", "dp_4")
    count = n_fsdp * n_near
    own = cols // count
    held = scatter_sum(inner_products(blended, projected, count), group)
    right_raw, gram = lax.optimization_barrier((held[:own], held[own:] * (1.0 / n_near)))
    summed, gram = lax.optimization_barrier((jnp.sum(gather(right_raw, far, n_dp // n_near), axis=0), gram))
    whole = gather(jnp.concatenate([summed, gram], axis=0), group, count)
    inverse_low, reduced, squares = whiten_right(whole, n_tensor)
    squares = lax.all_to_all(squares, "tensor", 0, 0)
    orthonormal, moment = left_and_moment(blended, projected, inverse_low, reduced)
    right_new, update = update_and_right(orthonormal, reduced, squares)
    return moment[None, None], right_new[None], update[None]


def solution(mesh):
    n_dp, n_fsdp, n_tensor = (mesh.shape[a] for a in ("dp", "fsdp", "tensor"))
    devices = mesh.devices.reshape(n_dp // 4, 2, 2, n_fsdp, n_tensor)
    mesh = jax.sharding.Mesh(devices, DP + ("fsdp", "tensor"))
    in_specs = (
        P(DP, None, "fsdp", "tensor"),
        P(DP, None, "fsdp", "tensor"),
        P(None, "tensor", None),
    )
    out_specs = (
        P(DP, None, "fsdp", "tensor"),
        P(None, "tensor", None),
        P(None, "fsdp", "tensor"),
    )
    return jax.shard_map(body, mesh=mesh, in_specs=in_specs, out_specs=out_specs, check_vma=False)
```

```python
import math

import jax
import jax.numpy as jnp
from jax import lax
from jax.experimental import pallas as pl
from jax.experimental.pallas import tpu as pltpu
from jax.sharding import PartitionSpec as P

M_ROWS = 7168
N_COLS = 2048
RANK = 128
SUB = 8
REPLICAS = 8


highest = lax.Precision.HIGHEST
decay_rate = 0.95
epsilon = 1e-06


def product(left, right):
    return jnp.dot(left, right, precision=highest, preferred_element_type=jnp.float32)


def inner_rows(left, right):
    return lax.dot_general(
        left, right, (((0,), (0,)), ((), ())), precision=highest, preferred_element_type=jnp.float32
    )


def outer_cols(left, right):
    return lax.dot_general(
        left, right, (((1,), (1,)), ((), ())), precision=highest, preferred_element_type=jnp.float32
    )


def terms(x):
    out = []
    for _ in range(3):
        out.append(x.astype(jnp.bfloat16))
        x = x - out[-1].astype(jnp.float32)
    return out


def dot(left, right):
    return jnp.dot(left, right, preferred_element_type=jnp.float32)


def spread(row):
    return jnp.broadcast_to(row, (SUB, RANK))


def far_product(left, right):
    l1, l2, l3 = terms(left)
    r1, r2, r3 = terms(right)
    return dot(jnp.concatenate([l1, l1, l2, l1, l3, l2], axis=1), jnp.concatenate([r1, r2, r1, r3, r1, r2], axis=0))


def invert_factor(tiles, write):
    lane = lax.broadcasted_iota(jnp.int32, (SUB, RANK), 1)
    sub = lax.broadcasted_iota(jnp.int32, (SUB, RANK), 0)
    count = len(tiles)
    for b in range(count):
        first = b * SUB
        panel = (lane >= first) & (lane < first + SUB)
        near, far = range(b, min(b + 3, count)), range(b + 3, count)
        columns = {
            t: [jnp.broadcast_to(tiles[t][:, first + k:first + k + 1], (SUB, RANK)) for k in range(SUB)] for t in near
        }
        pivot = [[spread(columns[b][j][k:k + 1]) if k >= j else None for k in range(SUB)] for j in range(SUB)]
        rows = [jnp.where(panel, (lane == first + p).astype(jnp.float32), spread(tiles[b][p:p + 1])) for p in range(SUB)]
        inverse = []
        for j in range(SUB):
            inverse.append(1.0 / pivot[j][j])
            for i in range(j + 1, SUB):
                ratio = pivot[j][i] * inverse[j]
                for k in range(i, SUB):
                    pivot[i][k] = pivot[i][k] - ratio * pivot[j][k]
                rows[i] = rows[i] - ratio * rows[j]
        for t in near[1:]:
            held = jnp.where(panel, 0.0, tiles[t])
            left = columns[t]
            for j in range(SUB):
                multiple = left[j] * inverse[j]
                for k in range(j + 1, SUB):
                    left[k] = left[k] - multiple * pivot[j][k]
                held = held - multiple * rows[j]
            tiles[t] = held
        if far:
            back = [None] * SUB
            for j in reversed(range(SUB)):
                row = rows[j]
                for k in range(j + 1, SUB):
                    row = row - pivot[j][k] * back[k]
                back[j] = row * inverse[j]
            block = back[0]
            for p in range(1, SUB):
                block = jnp.where(sub == p, back[p], block)
            zero = jnp.zeros((SUB, RANK), jnp.float32)
            block = jnp.concatenate([zero] * b + [block] + [zero] * (count - 1 - b), axis=0)
            taken = far_product(jnp.concatenate([tiles[t] for t in far], axis=0), block)
            for place, t in enumerate(far):
                tiles[t] = jnp.where(panel, 0.0, tiles[t]) - taken[place * SUB:(place + 1) * SUB]
        for p in range(SUB):
            d = pivot[p][p]
            root = lax.rsqrt(d)
            root = root * (1.5 - 0.5 * d * root * root)
            write(first + p, jnp.where(lane <= first + p, rows[p] * root, 0.0)[0:1])


def whiten_kernel(whole_ref, inverse_ref, reduced_ref, squares_ref):
    count, high, _ = whole_ref.shape
    share = RANK // count
    own = high - share
    tiles = [whole_ref[k, t:t + SUB] for k in range(count) for t in range(own, high, SUB)]

    def write(row, value):
        inverse_ref[row:row + 1, :] = value

    invert_factor(tiles, write)
    right_raw = jnp.concatenate([whole_ref[k, :own] for k in range(count)], axis=0)
    reduced = outer_cols(right_raw, inverse_ref[...]) * (1.0 / REPLICAS)
    reduced_ref[...] = reduced
    squares = jnp.sum(reduced * reduced, axis=0, keepdims=True)
    for k in range(squares_ref.shape[0]):
        squares_ref[k] = squares


def whiten_right(whole, n_tensor):
    count, high, _ = whole.shape
    cols = count * high - RANK
    vmem = pl.BlockSpec(memory_space=pltpu.VMEM)
    return pl.pallas_call(
        whiten_kernel,
        out_shape=(
            jax.ShapeDtypeStruct((RANK, RANK), jnp.float32),
            jax.ShapeDtypeStruct((cols, RANK), jnp.float32),
            jax.ShapeDtypeStruct((n_tensor, 1, RANK), jnp.float32),
        ),
        in_specs=[vmem],
        out_specs=[vmem] * 3,
        compiler_params=pltpu.CompilerParams(vmem_limit_bytes=16 * 2**20),
    )(whole)


def inner_kernel(blended_ref, projected_ref, out_ref):
    count, share = out_ref.shape[0], RANK // out_ref.shape[0]
    own = out_ref.shape[1] - share
    cols = count * own
    projected = projected_ref[...]
    r1, r2, r3 = terms(projected)
    l1, l2, l3 = terms(jnp.concatenate([blended_ref[...], projected], axis=1).T)
    pair = jnp.concatenate([r1, r2], axis=1)
    high, low = dot(l1, pair), dot(l2, pair)
    rest = low[:, RANK:] + (dot(l1, r3) + dot(l3, r1))
    both = high[:, :RANK] + ((high[:, RANK:] + low[:, :RANK]) + rest)
    for k in range(count):
        out_ref[k, :own] = both[k * own:(k + 1) * own]
        out_ref[k, own:] = both[cols + k * share:cols + (k + 1) * share]


def inner_products(blended, projected, count):
    rows, cols = blended.shape
    vmem = pl.BlockSpec(memory_space=pltpu.VMEM)
    return pl.pallas_call(
        inner_kernel,
        out_shape=jax.ShapeDtypeStruct((count, (cols + RANK) // count, RANK), jnp.float32),
        in_specs=[vmem] * 2,
        out_specs=vmem,
        compiler_params=pltpu.CompilerParams(vmem_limit_bytes=24 * 2**20),
    )(blended, projected)


def halves(x):
    high = x.astype(jnp.bfloat16)
    return high, (x - high.astype(jnp.float32)).astype(jnp.bfloat16)


def outer_of_halves(left, right):
    def outer(left, right):
        return lax.dot_general(left, right, (((1,), (1,)), ((), ())), preferred_element_type=jnp.float32)

    return outer(left[0], right[0]) + (outer(left[0], right[1]) + outer(left[1], right[0]))


def moment_kernel(blended_ref, projected_ref, inverse_ref, reduced_ref, left_ref, moment_out, moment_ref, sems):
    steps = sems.shape[0]
    rows = left_ref.shape[0] // steps
    inverse = inverse_ref[...]
    right = halves(reduced_ref[...] * (1.0 - decay_rate))
    copies = []
    for step in range(steps):
        block = pl.ds(step * rows, rows)
        left = outer_cols(projected_ref[block, :], inverse)
        left_ref[block, :] = left
        moment_ref[block, :] = blended_ref[block, :] - outer_of_halves(halves(left), right)
        copies.append(pltpu.make_async_copy(moment_ref.at[block], moment_out.at[block], sems.at[step]))
        copies[-1].start()
    for copy in copies:
        copy.wait()


def left_and_moment(blended, projected, inverse_low, reduced):
    steps = 4
    rows, cols = blended.shape
    vmem, anywhere = pl.BlockSpec(memory_space=pltpu.VMEM), pl.BlockSpec(memory_space=pl.ANY)
    return pl.pallas_call(
        moment_kernel,
        out_shape=(
            jax.ShapeDtypeStruct((rows, RANK), jnp.float32),
            jax.ShapeDtypeStruct((rows, cols), jnp.float32),
        ),
        in_specs=[vmem] * 4,
        out_specs=[vmem, anywhere],
        scratch_shapes=[pltpu.VMEM((rows, cols), jnp.float32), pltpu.SemaphoreType.DMA((steps,))],
        compiler_params=pltpu.CompilerParams(vmem_limit_bytes=24 * 2**20),
        cost_estimate=pl.CostEstimate(
            flops=12 * rows * cols * RANK, bytes_accessed=4 * rows * cols, transcendentals=0
        ),
    )(blended, projected, inverse_low, reduced)


def update_kernel(left_ref, reduced_ref, squares_ref, right_out, update_out, right_ref, update_ref, sems):
    steps = sems.shape[0] - 1
    rows = left_ref.shape[0] // steps

    norm = jnp.sqrt(jnp.sum(squares_ref[...], axis=0)) + epsilon
    right_new = reduced_ref[...] / norm
    right_ref[...] = right_new
    copies = [pltpu.make_async_copy(right_ref, right_out, sems.at[steps])]
    copies[0].start()
    right = halves(right_new * math.sqrt(M_ROWS * N_COLS / RANK))
    for step in range(steps):
        block = pl.ds(step * rows, rows)
        update_ref[block, :] = outer_of_halves(halves(left_ref[block, :]), right).astype(jnp.bfloat16)
        copies.append(pltpu.make_async_copy(update_ref.at[block], update_out.at[block], sems.at[step]))
        copies[-1].start()
    for copy in copies:
        copy.wait()


def update_and_right(left, reduced, squares):
    steps = 4
    rows, cols = left.shape[0], reduced.shape[0]
    vmem, anywhere = pl.BlockSpec(memory_space=pltpu.VMEM), pl.BlockSpec(memory_space=pl.ANY)
    return pl.pallas_call(
        update_kernel,
        out_shape=(
            jax.ShapeDtypeStruct((cols, RANK), jnp.float32),
            jax.ShapeDtypeStruct((rows, cols), jnp.bfloat16),
        ),
        in_specs=[vmem] * 3,
        out_specs=[anywhere] * 2,
        scratch_shapes=[
            pltpu.VMEM((cols, RANK), jnp.float32),
            pltpu.VMEM((rows, cols), jnp.bfloat16),
            pltpu.SemaphoreType.DMA((steps + 1,)),
        ],
        compiler_params=pltpu.CompilerParams(vmem_limit_bytes=16 * 2**20),
    )(left, reduced, squares)


def scatter_sum(blocks, axes):
    return jnp.sum(lax.all_to_all(blocks, axes, 0, 0), axis=0)


def gather(block, axes, count):
    return lax.all_to_all(jnp.broadcast_to(block, (count,) + block.shape), axes, 0, 0)


def body(momentum, gradient, right_factor):
    n_far, n_near, n_fsdp, n_tensor = (lax.axis_size(a) for a in ("dp_far", "dp_near", "fsdp", "tensor"))
    blended = momentum[0, 0] + gradient[0, 0].astype(jnp.float32)
    rows, cols = blended.shape
    plane = ("dp_far", "dp_near", "tensor")
    count = n_far * n_near * n_tensor
    blocks, lines = (count, rows // count, RANK), (count, 1, rows // count * RANK)
    partial = lax.optimization_barrier(product(blended, right_factor[0]))
    parts = lax.all_to_all(partial.reshape(lines), plane, 0, 0).reshape(rows, RANK)
    part = jnp.sum(lax.optimization_barrier(parts).reshape(blocks), axis=0)
    copies = lax.optimization_barrier(jnp.broadcast_to(part, blocks).reshape(rows, RANK))
    projected = lax.all_to_all(copies.reshape(lines), plane, 0, 0).reshape(rows, RANK)
    group = ("fsdp", "dp_near")
    count = n_fsdp * n_near
    own = cols // count
    held = scatter_sum(inner_products(blended, projected, count), group)
    right_raw, gram = lax.optimization_barrier((held[:own], held[own:] * (1.0 / n_near)))
    summed, gram = lax.optimization_barrier((jnp.sum(gather(right_raw, "dp_far", n_far), axis=0), gram))
    whole = gather(jnp.concatenate([summed, gram], axis=0), group, count)
    inverse_low, reduced, squares = whiten_right(whole, n_tensor)
    squares = lax.all_to_all(squares, "tensor", 0, 0)
    orthonormal, moment = left_and_moment(blended, projected, inverse_low, reduced)
    right_new, update = update_and_right(orthonormal, reduced, squares)
    return moment[None, None], right_new[None], update[None]


def solution(mesh):
    near = 2
    n_dp, n_fsdp, n_tensor = (mesh.shape[a] for a in ("dp", "fsdp", "tensor"))
    devices = mesh.devices.reshape(n_dp // near, near, n_fsdp, n_tensor)
    mesh = jax.sharding.Mesh(devices, ("dp_far", "dp_near", "fsdp", "tensor"))
    dp = ("dp_far", "dp_near")
    in_specs = (
        P(dp, None, "fsdp", "tensor"),
        P(dp, None, "fsdp", "tensor"),
        P(None, "tensor", None),
    )
    out_specs = (
        P(dp, None, "fsdp", "tensor"),
        P(None, "tensor", None),
        P(None, "fsdp", "tensor"),
    )
    return jax.shard_map(body, mesh=mesh, in_specs=in_specs, out_specs=out_specs, check_vma=False)
```

```python
import math

import jax
import jax.numpy as jnp
from jax import lax
from jax.experimental import pallas as pl
from jax.experimental.pallas import tpu as pltpu
from jax.sharding import PartitionSpec as P

M_ROWS = 7168
N_COLS = 2048
RANK = 128
SUB = 8
REPLICAS = 8


highest = lax.Precision.HIGHEST
decay_rate = 0.95
epsilon = 1e-06


def outer_cols(left, right):
    return lax.dot_general(
        left, right, (((1,), (1,)), ((), ())), precision=highest, preferred_element_type=jnp.float32
    )


def terms(x):
    out = []
    for _ in range(3):
        out.append(x.astype(jnp.bfloat16))
        x = x - out[-1].astype(jnp.float32)
    return out


def dot(left, right):
    return jnp.dot(left, right, preferred_element_type=jnp.float32)


def six_products(left, right):
    l1, l2, l3 = left
    r1, r2, r3 = right
    pair = jnp.concatenate([r1, r2], axis=1)
    high, low = dot(l1, pair), dot(l2, pair)
    rest = low[:, RANK:] + (dot(l1, r3) + dot(l3, r1))
    return high[:, :RANK] + ((high[:, RANK:] + low[:, :RANK]) + rest)


def spread(row):
    return jnp.broadcast_to(row, (SUB, RANK))


def far_product(left, right):
    l1, l2, l3 = terms(left)
    r1, r2, r3 = terms(right)
    return dot(jnp.concatenate([l1, l1, l2, l1, l3, l2], axis=1), jnp.concatenate([r1, r2, r1, r3, r1, r2], axis=0))


def invert_factor(tiles, write):
    lane = lax.broadcasted_iota(jnp.int32, (SUB, RANK), 1)
    sub = lax.broadcasted_iota(jnp.int32, (SUB, RANK), 0)
    count = len(tiles)
    for b in range(count):
        first = b * SUB
        panel = (lane >= first) & (lane < first + SUB)
        near, far = range(b, min(b + 3, count)), range(b + 3, count)
        columns = {
            t: [jnp.broadcast_to(tiles[t][:, first + k:first + k + 1], (SUB, RANK)) for k in range(SUB)] for t in near
        }
        pivot = [[spread(columns[b][j][k:k + 1]) if k >= j else None for k in range(SUB)] for j in range(SUB)]
        rows = [jnp.where(panel, (lane == first + p).astype(jnp.float32), spread(tiles[b][p:p + 1])) for p in range(SUB)]
        inverse = []
        for j in range(SUB):
            inverse.append(1.0 / pivot[j][j])
            for i in range(j + 1, SUB):
                ratio = pivot[j][i] * inverse[j]
                for k in range(i, SUB):
                    pivot[i][k] = pivot[i][k] - ratio * pivot[j][k]
                rows[i] = rows[i] - ratio * rows[j]
        for t in near[1:]:
            held = jnp.where(panel, 0.0, tiles[t])
            left = columns[t]
            for j in range(SUB):
                multiple = left[j] * inverse[j]
                for k in range(j + 1, SUB):
                    left[k] = left[k] - multiple * pivot[j][k]
                held = held - multiple * rows[j]
            tiles[t] = held
        if far:
            back = [None] * SUB
            for j in reversed(range(SUB)):
                row = rows[j]
                for k in range(j + 1, SUB):
                    row = row - pivot[j][k] * back[k]
                back[j] = row * inverse[j]
            block = back[0]
            for p in range(1, SUB):
                block = jnp.where(sub == p, back[p], block)
            zero = jnp.zeros((SUB, RANK), jnp.float32)
            block = jnp.concatenate([zero] * b + [block] + [zero] * (count - 1 - b), axis=0)
            taken = far_product(jnp.concatenate([tiles[t] for t in far], axis=0), block)
            for place, t in enumerate(far):
                tiles[t] = jnp.where(panel, 0.0, tiles[t]) - taken[place * SUB:(place + 1) * SUB]
        for p in range(SUB):
            d = pivot[p][p]
            root = lax.rsqrt(d)
            root = root * (1.5 - 0.5 * d * root * root)
            write(first + p, jnp.where(lane <= first + p, rows[p] * root, 0.0)[0:1])


def whiten_kernel(whole_ref, inverse_ref, reduced_ref, squares_ref):
    count, high, _ = whole_ref.shape
    share = RANK // count
    own = high - share
    tiles = [whole_ref[k, t:t + SUB] for k in range(count) for t in range(own, high, SUB)]

    def write(row, value):
        inverse_ref[row:row + 1, :] = value

    invert_factor(tiles, write)
    right_raw = jnp.concatenate([whole_ref[k, :own] for k in range(count)], axis=0)
    reduced = outer_cols(right_raw, inverse_ref[...]) * (1.0 / REPLICAS)
    reduced_ref[...] = reduced
    squares = jnp.sum(reduced * reduced, axis=0, keepdims=True)
    for k in range(squares_ref.shape[0]):
        squares_ref[k] = squares


def whiten_right(whole, n_tensor):
    count, high, _ = whole.shape
    cols = count * high - RANK
    vmem = pl.BlockSpec(memory_space=pltpu.VMEM)
    return pl.pallas_call(
        whiten_kernel,
        out_shape=(
            jax.ShapeDtypeStruct((RANK, RANK), jnp.float32),
            jax.ShapeDtypeStruct((cols, RANK), jnp.float32),
            jax.ShapeDtypeStruct((n_tensor, 1, RANK), jnp.float32),
        ),
        in_specs=[vmem],
        out_specs=[vmem] * 3,
        compiler_params=pltpu.CompilerParams(vmem_limit_bytes=16 * 2**20),
    )(whole)


def project_kernel(blended_ref, right_ref, out_ref):
    out_ref[...] = six_products(terms(blended_ref[...]), terms(right_ref[...]))


def project(blended, right):
    vmem = pl.BlockSpec(memory_space=pltpu.VMEM)
    return pl.pallas_call(
        project_kernel,
        out_shape=jax.ShapeDtypeStruct((blended.shape[0], RANK), jnp.float32),
        in_specs=[vmem] * 2,
        out_specs=vmem,
        compiler_params=pltpu.CompilerParams(vmem_limit_bytes=24 * 2**20),
    )(blended, right)


def inner_kernel(blended_ref, projected_ref, out_ref):
    count, share = out_ref.shape[0], RANK // out_ref.shape[0]
    own = out_ref.shape[1] - share
    cols = count * own
    projected = projected_ref[...]
    both = six_products(terms(jnp.concatenate([blended_ref[...], projected], axis=1).T), terms(projected))
    for k in range(count):
        out_ref[k, :own] = both[k * own:(k + 1) * own]
        out_ref[k, own:] = both[cols + k * share:cols + (k + 1) * share]


def inner_products(blended, projected, count):
    rows, cols = blended.shape
    vmem = pl.BlockSpec(memory_space=pltpu.VMEM)
    return pl.pallas_call(
        inner_kernel,
        out_shape=jax.ShapeDtypeStruct((count, (cols + RANK) // count, RANK), jnp.float32),
        in_specs=[vmem] * 2,
        out_specs=vmem,
        compiler_params=pltpu.CompilerParams(vmem_limit_bytes=24 * 2**20),
    )(blended, projected)


def halves(x):
    high = x.astype(jnp.bfloat16)
    return high, (x - high.astype(jnp.float32)).astype(jnp.bfloat16)


def outer_of_halves(left, right):
    def outer(left, right):
        return lax.dot_general(left, right, (((1,), (1,)), ((), ())), preferred_element_type=jnp.float32)

    return outer(left[0], right[0]) + (outer(left[0], right[1]) + outer(left[1], right[0]))


def moment_kernel(blended_ref, projected_ref, inverse_ref, reduced_ref, left_ref, moment_out, moment_ref, sems):
    steps = sems.shape[0]
    rows = left_ref.shape[0] // steps
    inverse = inverse_ref[...]
    right = halves(reduced_ref[...] * (1.0 - decay_rate))
    copies = []
    for step in range(steps):
        block = pl.ds(step * rows, rows)
        left = outer_cols(projected_ref[block, :], inverse)
        left_ref[block, :] = left
        moment_ref[block, :] = blended_ref[block, :] - outer_of_halves(halves(left), right)
        copies.append(pltpu.make_async_copy(moment_ref.at[block], moment_out.at[block], sems.at[step]))
        copies[-1].start()
    for copy in copies:
        copy.wait()


def left_and_moment(blended, projected, inverse_low, reduced):
    steps = 4
    rows, cols = blended.shape
    vmem, anywhere = pl.BlockSpec(memory_space=pltpu.VMEM), pl.BlockSpec(memory_space=pl.ANY)
    return pl.pallas_call(
        moment_kernel,
        out_shape=(
            jax.ShapeDtypeStruct((rows, RANK), jnp.float32),
            jax.ShapeDtypeStruct((rows, cols), jnp.float32),
        ),
        in_specs=[vmem] * 4,
        out_specs=[vmem, anywhere],
        scratch_shapes=[pltpu.VMEM((rows, cols), jnp.float32), pltpu.SemaphoreType.DMA((steps,))],
        compiler_params=pltpu.CompilerParams(vmem_limit_bytes=24 * 2**20),
        cost_estimate=pl.CostEstimate(
            flops=12 * rows * cols * RANK, bytes_accessed=4 * rows * cols, transcendentals=0
        ),
    )(blended, projected, inverse_low, reduced)


def update_kernel(left_ref, reduced_ref, squares_ref, right_out, update_out, right_ref, update_ref, sems):
    steps = sems.shape[0] - 1
    rows = left_ref.shape[0] // steps

    norm = jnp.sqrt(jnp.sum(squares_ref[...], axis=0)) + epsilon
    right_new = reduced_ref[...] / norm
    right_ref[...] = right_new
    copies = [pltpu.make_async_copy(right_ref, right_out, sems.at[steps])]
    copies[0].start()
    right = halves(right_new * math.sqrt(M_ROWS * N_COLS / RANK))
    for step in range(steps):
        block = pl.ds(step * rows, rows)
        update_ref[block, :] = outer_of_halves(halves(left_ref[block, :]), right).astype(jnp.bfloat16)
        copies.append(pltpu.make_async_copy(update_ref.at[block], update_out.at[block], sems.at[step]))
        copies[-1].start()
    for copy in copies:
        copy.wait()


def update_and_right(left, reduced, squares):
    steps = 4
    rows, cols = left.shape[0], reduced.shape[0]
    vmem, anywhere = pl.BlockSpec(memory_space=pltpu.VMEM), pl.BlockSpec(memory_space=pl.ANY)
    return pl.pallas_call(
        update_kernel,
        out_shape=(
            jax.ShapeDtypeStruct((cols, RANK), jnp.float32),
            jax.ShapeDtypeStruct((rows, cols), jnp.bfloat16),
        ),
        in_specs=[vmem] * 3,
        out_specs=[anywhere] * 2,
        scratch_shapes=[
            pltpu.VMEM((cols, RANK), jnp.float32),
            pltpu.VMEM((rows, cols), jnp.bfloat16),
            pltpu.SemaphoreType.DMA((steps + 1,)),
        ],
        compiler_params=pltpu.CompilerParams(vmem_limit_bytes=16 * 2**20),
    )(left, reduced, squares)


def scatter_sum(blocks, axes):
    return jnp.sum(lax.all_to_all(blocks, axes, 0, 0), axis=0)


def gather(block, axes, count):
    return lax.all_to_all(jnp.broadcast_to(block, (count,) + block.shape), axes, 0, 0)


def body(momentum, gradient, right_factor):
    n_far, n_near, n_fsdp, n_tensor = (lax.axis_size(a) for a in ("dp_far", "dp_near", "fsdp", "tensor"))
    blended = momentum[0, 0] + gradient[0, 0].astype(jnp.float32)
    rows, cols = blended.shape
    plane = ("dp_far", "dp_near", "tensor")
    count = n_far * n_near * n_tensor
    blocks, lines = (count, rows // count, RANK), (count, 1, rows // count * RANK)
    partial = lax.optimization_barrier(project(blended, right_factor[0]))
    parts = lax.all_to_all(partial.reshape(lines), plane, 0, 0).reshape(rows, RANK)
    part = jnp.sum(lax.optimization_barrier(parts).reshape(blocks), axis=0)
    copies = lax.optimization_barrier(jnp.broadcast_to(part, blocks).reshape(rows, RANK))
    projected = lax.all_to_all(copies.reshape(lines), plane, 0, 0).reshape(rows, RANK)
    group = ("fsdp", "dp_near")
    count = n_fsdp * n_near
    own = cols // count
    held = scatter_sum(inner_products(blended, projected, count), group)
    right_raw, gram = lax.optimization_barrier((held[:own], held[own:] * (1.0 / n_near)))
    summed, gram = lax.optimization_barrier((jnp.sum(gather(right_raw, "dp_far", n_far), axis=0), gram))
    whole = gather(jnp.concatenate([summed, gram], axis=0), group, count)
    inverse_low, reduced, squares = whiten_right(whole, n_tensor)
    squares = lax.all_to_all(squares, "tensor", 0, 0)
    orthonormal, moment = left_and_moment(blended, projected, inverse_low, reduced)
    right_new, update = update_and_right(orthonormal, reduced, squares)
    return moment[None, None], right_new[None], update[None]


def solution(mesh):
    near = 2
    n_dp, n_fsdp, n_tensor = (mesh.shape[a] for a in ("dp", "fsdp", "tensor"))
    devices = mesh.devices.reshape(n_dp // near, near, n_fsdp, n_tensor)
    mesh = jax.sharding.Mesh(devices, ("dp_far", "dp_near", "fsdp", "tensor"))
    dp = ("dp_far", "dp_near")
    in_specs = (
        P(dp, None, "fsdp", "tensor"),
        P(dp, None, "fsdp", "tensor"),
        P(None, "tensor", None),
    )
    out_specs = (
        P(dp, None, "fsdp", "tensor"),
        P(None, "tensor", None),
        P(None, "fsdp", "tensor"),
    )
    return jax.shard_map(body, mesh=mesh, in_specs=in_specs, out_specs=out_specs, check_vma=False)
```

```python
import math

import jax
import jax.numpy as jnp
from jax import lax
from jax.experimental import pallas as pl
from jax.experimental.pallas import tpu as pltpu
from jax.sharding import PartitionSpec as P

M_ROWS = 7168
N_COLS = 2048
RANK = 128
SUB = 8
REPLICAS = 8


highest = lax.Precision.HIGHEST
decay_rate = 0.95
epsilon = 1e-06


def outer_cols(left, right):
    return lax.dot_general(
        left, right, (((1,), (1,)), ((), ())), precision=highest, preferred_element_type=jnp.float32
    )


def terms(x):
    out = []
    for _ in range(3):
        out.append(x.astype(jnp.bfloat16))
        x = x - out[-1].astype(jnp.float32)
    return out


def dot(left, right):
    return jnp.dot(left, right, preferred_element_type=jnp.float32)


def six_products(left, right):
    l1, l2, l3 = left
    r1, r2, r3 = right
    pair = jnp.concatenate([r1, r2], axis=1)
    high, low = dot(l1, pair), dot(l2, pair)
    rest = low[:, RANK:] + (dot(l1, r3) + dot(l3, r1))
    return high[:, :RANK] + ((high[:, RANK:] + low[:, :RANK]) + rest)


def spread(row):
    return jnp.broadcast_to(row, (SUB, RANK))


def far_product(left, right):
    l1, l2, l3 = terms(left)
    r1, r2, r3 = terms(right)
    return dot(jnp.concatenate([l1, l1, l2, l1, l3, l2], axis=1), jnp.concatenate([r1, r2, r1, r3, r1, r2], axis=0))


def invert_factor(tiles, write):
    lane = lax.broadcasted_iota(jnp.int32, (SUB, RANK), 1)
    sub = lax.broadcasted_iota(jnp.int32, (SUB, RANK), 0)
    count = len(tiles)
    for b in range(count):
        first = b * SUB
        panel = (lane >= first) & (lane < first + SUB)
        near, far = range(b, min(b + 3, count)), range(b + 3, count)
        columns = {
            t: [jnp.broadcast_to(tiles[t][:, first + k:first + k + 1], (SUB, RANK)) for k in range(SUB)] for t in near
        }
        pivot = [[spread(columns[b][j][k:k + 1]) if k >= j else None for k in range(SUB)] for j in range(SUB)]
        rows = [jnp.where(panel, (lane == first + p).astype(jnp.float32), spread(tiles[b][p:p + 1])) for p in range(SUB)]
        inverse = []
        for j in range(SUB):
            inverse.append(1.0 / pivot[j][j])
            for i in range(j + 1, SUB):
                ratio = pivot[j][i] * inverse[j]
                for k in range(i, SUB):
                    pivot[i][k] = pivot[i][k] - ratio * pivot[j][k]
                rows[i] = rows[i] - ratio * rows[j]
        for t in near[1:]:
            held = jnp.where(panel, 0.0, tiles[t])
            left = columns[t]
            for j in range(SUB):
                multiple = left[j] * inverse[j]
                for k in range(j + 1, SUB):
                    left[k] = left[k] - multiple * pivot[j][k]
                held = held - multiple * rows[j]
            tiles[t] = held
        if far:
            back = [None] * SUB
            for j in reversed(range(SUB)):
                row = rows[j]
                for k in range(j + 1, SUB):
                    row = row - pivot[j][k] * back[k]
                back[j] = row * inverse[j]
            block = back[0]
            for p in range(1, SUB):
                block = jnp.where(sub == p, back[p], block)
            zero = jnp.zeros((SUB, RANK), jnp.float32)
            block = jnp.concatenate([zero] * b + [block] + [zero] * (count - 1 - b), axis=0)
            taken = far_product(jnp.concatenate([tiles[t] for t in far], axis=0), block)
            for place, t in enumerate(far):
                tiles[t] = jnp.where(panel, 0.0, tiles[t]) - taken[place * SUB:(place + 1) * SUB]
        for p in range(SUB):
            d = pivot[p][p]
            root = lax.rsqrt(d)
            root = root * (1.5 - 0.5 * d * root * root)
            write(first + p, jnp.where(lane <= first + p, rows[p] * root, 0.0)[0:1])


def whiten_kernel(whole_ref, inverse_ref, reduced_ref, squares_ref):
    count, high, _ = whole_ref.shape
    share = RANK // count
    own = high - share
    tiles = [whole_ref[k, t:t + SUB] for k in range(count) for t in range(own, high, SUB)]

    def write(row, value):
        inverse_ref[row:row + 1, :] = value

    invert_factor(tiles, write)
    right_raw = jnp.concatenate([whole_ref[k, :own] for k in range(count)], axis=0)
    reduced = outer_cols(right_raw, inverse_ref[...]) * (1.0 / REPLICAS)
    reduced_ref[...] = reduced
    squares = jnp.sum(reduced * reduced, axis=0, keepdims=True)
    for k in range(squares_ref.shape[0]):
        squares_ref[k] = squares


def whiten_right(whole, n_tensor):
    count, high, _ = whole.shape
    cols = count * high - RANK
    vmem = pl.BlockSpec(memory_space=pltpu.VMEM)
    return pl.pallas_call(
        whiten_kernel,
        out_shape=(
            jax.ShapeDtypeStruct((RANK, RANK), jnp.float32),
            jax.ShapeDtypeStruct((cols, RANK), jnp.float32),
            jax.ShapeDtypeStruct((n_tensor, 1, RANK), jnp.float32),
        ),
        in_specs=[vmem],
        out_specs=[vmem] * 3,
        compiler_params=pltpu.CompilerParams(vmem_limit_bytes=16 * 2**20),
    )(whole)


def project_kernel(blended_ref, right_ref, out_ref):
    out_ref[...] = six_products(terms(blended_ref[...]), terms(right_ref[...]))


def project(blended, right):
    vmem = pl.BlockSpec(memory_space=pltpu.VMEM)
    return pl.pallas_call(
        project_kernel,
        out_shape=jax.ShapeDtypeStruct((blended.shape[0], RANK), jnp.float32),
        in_specs=[vmem] * 2,
        out_specs=vmem,
        compiler_params=pltpu.CompilerParams(vmem_limit_bytes=24 * 2**20),
    )(blended, right)


def inner_kernel(blended_ref, projected_ref, out_ref):
    count, share = out_ref.shape[0], RANK // out_ref.shape[0]
    own = out_ref.shape[1] - share
    cols = count * own
    projected = projected_ref[...]
    both = six_products(terms(jnp.concatenate([blended_ref[...], projected], axis=1).T), terms(projected))
    for k in range(count):
        out_ref[k, :own] = both[k * own:(k + 1) * own]
        out_ref[k, own:] = both[cols + k * share:cols + (k + 1) * share]


def inner_products(blended, projected, count):
    rows, cols = blended.shape
    vmem = pl.BlockSpec(memory_space=pltpu.VMEM)
    return pl.pallas_call(
        inner_kernel,
        out_shape=jax.ShapeDtypeStruct((count, (cols + RANK) // count, RANK), jnp.float32),
        in_specs=[vmem] * 2,
        out_specs=vmem,
        compiler_params=pltpu.CompilerParams(vmem_limit_bytes=24 * 2**20),
    )(blended, projected)


def halves(x):
    high = x.astype(jnp.bfloat16)
    return high, (x - high.astype(jnp.float32)).astype(jnp.bfloat16)


def outer_of_halves(left, right):
    def outer(left, right):
        return lax.dot_general(left, right, (((1,), (1,)), ((), ())), preferred_element_type=jnp.float32)

    return outer(left[0], right[0]) + (outer(left[0], right[1]) + outer(left[1], right[0]))


def moment_kernel(blended_ref, projected_ref, inverse_ref, reduced_ref, left_ref, moment_out, moment_ref, sems):
    steps = sems.shape[0]
    rows = left_ref.shape[0] // steps
    inverse = inverse_ref[...]
    right = halves(reduced_ref[...] * (1.0 - decay_rate))
    copies = []
    for step in range(steps):
        block = pl.ds(step * rows, rows)
        left = outer_cols(projected_ref[block, :], inverse)
        left_ref[block, :] = left
        moment_ref[block, :] = blended_ref[block, :] - outer_of_halves(halves(left), right)
        copies.append(pltpu.make_async_copy(moment_ref.at[block], moment_out.at[block], sems.at[step]))
        copies[-1].start()
    for copy in copies:
        copy.wait()


def left_and_moment(blended, projected, inverse_low, reduced):
    steps = 4
    rows, cols = blended.shape
    vmem, anywhere = pl.BlockSpec(memory_space=pltpu.VMEM), pl.BlockSpec(memory_space=pl.ANY)
    return pl.pallas_call(
        moment_kernel,
        out_shape=(
            jax.ShapeDtypeStruct((rows, RANK), jnp.float32),
            jax.ShapeDtypeStruct((rows, cols), jnp.float32),
        ),
        in_specs=[vmem] * 4,
        out_specs=[vmem, anywhere],
        scratch_shapes=[pltpu.VMEM((rows, cols), jnp.float32), pltpu.SemaphoreType.DMA((steps,))],
        compiler_params=pltpu.CompilerParams(vmem_limit_bytes=24 * 2**20),
        cost_estimate=pl.CostEstimate(
            flops=12 * rows * cols * RANK, bytes_accessed=4 * rows * cols, transcendentals=0
        ),
    )(blended, projected, inverse_low, reduced)


def update_kernel(left_ref, reduced_ref, squares_ref, right_out, update_out, right_ref, update_ref, sems):
    steps = sems.shape[0] - 1
    rows = left_ref.shape[0] // steps

    norm = jnp.sqrt(jnp.sum(squares_ref[...], axis=0)) + epsilon
    right_new = reduced_ref[...] / norm
    right_ref[...] = right_new
    copies = [pltpu.make_async_copy(right_ref, right_out, sems.at[steps])]
    copies[0].start()
    right = halves(right_new * math.sqrt(M_ROWS * N_COLS / RANK))
    for step in range(steps):
        block = pl.ds(step * rows, rows)
        update_ref[block, :] = outer_of_halves(halves(left_ref[block, :]), right).astype(jnp.bfloat16)
        copies.append(pltpu.make_async_copy(update_ref.at[block], update_out.at[block], sems.at[step]))
        copies[-1].start()
    for copy in copies:
        copy.wait()


def update_and_right(left, reduced, squares):
    steps = 4
    rows, cols = left.shape[0], reduced.shape[0]
    vmem, anywhere = pl.BlockSpec(memory_space=pltpu.VMEM), pl.BlockSpec(memory_space=pl.ANY)
    return pl.pallas_call(
        update_kernel,
        out_shape=(
            jax.ShapeDtypeStruct((cols, RANK), jnp.float32),
            jax.ShapeDtypeStruct((rows, cols), jnp.bfloat16),
        ),
        in_specs=[vmem] * 3,
        out_specs=[anywhere] * 2,
        scratch_shapes=[
            pltpu.VMEM((cols, RANK), jnp.float32),
            pltpu.VMEM((rows, cols), jnp.bfloat16),
            pltpu.SemaphoreType.DMA((steps + 1,)),
        ],
        compiler_params=pltpu.CompilerParams(vmem_limit_bytes=16 * 2**20),
    )(left, reduced, squares)


def scatter_sum(blocks, axes):
    return jnp.sum(lax.all_to_all(blocks, axes, 0, 0), axis=0)


def gather(block, axes, count):
    return lax.all_to_all(jnp.broadcast_to(block, (count,) + block.shape), axes, 0, 0)


def body(momentum, gradient, right_factor):
    n_far, n_near, n_fsdp, n_tensor = (lax.axis_size(a) for a in ("dp_far", "dp_near", "fsdp", "tensor"))
    blended = momentum[0, 0] + gradient[0, 0].astype(jnp.float32)
    rows, cols = blended.shape
    plane = ("dp_far", "dp_near", "tensor")
    count = n_far * n_near * n_tensor
    blocks, lines = (count, rows // count, RANK), (count, 1, rows // count * RANK)
    partial = lax.optimization_barrier(project(blended, right_factor[0]))
    parts = lax.all_to_all(partial.reshape(lines), plane, 0, 0).reshape(rows, RANK)
    part = jnp.sum(lax.optimization_barrier(parts).reshape(blocks), axis=0)
    copies = lax.optimization_barrier(jnp.broadcast_to(part, blocks).reshape(rows, RANK))
    projected = lax.all_to_all(copies.reshape(lines), plane, 0, 0).reshape(rows, RANK)
    group = ("dp_near", "fsdp")
    count = n_fsdp * n_near
    own = cols // count
    held = scatter_sum(inner_products(blended, projected, count), group)
    right_raw, gram = lax.optimization_barrier((held[:own], held[own:] * (1.0 / n_near)))
    summed, gram = lax.optimization_barrier((jnp.sum(gather(right_raw, "dp_far", n_far), axis=0), gram))
    whole = gather(jnp.concatenate([summed, gram], axis=0), group, count)
    inverse_low, reduced, squares = whiten_right(whole, n_tensor)
    squares = lax.all_to_all(squares, "tensor", 0, 0)
    orthonormal, moment = left_and_moment(blended, projected, inverse_low, reduced)
    right_new, update = update_and_right(orthonormal, reduced, squares)
    return moment[None, None], right_new[None], update[None]


def solution(mesh):
    near = 2
    n_dp, n_fsdp, n_tensor = (mesh.shape[a] for a in ("dp", "fsdp", "tensor"))
    devices = mesh.devices.reshape(n_dp // near, near, n_fsdp, n_tensor)
    mesh = jax.sharding.Mesh(devices, ("dp_far", "dp_near", "fsdp", "tensor"))
    dp = ("dp_far", "dp_near")
    in_specs = (
        P(dp, None, "fsdp", "tensor"),
        P(dp, None, "fsdp", "tensor"),
        P(None, "tensor", None),
    )
    out_specs = (
        P(dp, None, "fsdp", "tensor"),
        P(None, "tensor", None),
        P(None, "fsdp", "tensor"),
    )
    return jax.shard_map(body, mesh=mesh, in_specs=in_specs, out_specs=out_specs, check_vma=False)
```

```python
import functools
import math

import jax
import jax.numpy as jnp
from jax import lax
from jax.experimental import pallas as pl
from jax.experimental.pallas import tpu as pltpu
from jax.sharding import PartitionSpec as P

M_ROWS = 7168
N_COLS = 2048
RANK = 128
SUB = 8
REPLICAS = 8


highest = lax.Precision.HIGHEST
decay_rate = 0.95
epsilon = 1e-06


def outer_cols(left, right):
    return lax.dot_general(
        left, right, (((1,), (1,)), ((), ())), precision=highest, preferred_element_type=jnp.float32
    )


def terms(x):
    out = []
    for _ in range(3):
        out.append(x.astype(jnp.bfloat16))
        x = x - out[-1].astype(jnp.float32)
    return out


def dot(left, right):
    return jnp.dot(left, right, preferred_element_type=jnp.float32)


def six_products(left, right):
    l1, l2, l3 = left
    r1, r2, r3 = right
    pair = jnp.concatenate([r1, r2], axis=1)
    high, low = dot(l1, pair), dot(l2, pair)
    rest = low[:, RANK:] + (dot(l1, r3) + dot(l3, r1))
    return high[:, :RANK] + ((high[:, RANK:] + low[:, :RANK]) + rest)


def spread(row):
    return jnp.broadcast_to(row, (SUB, RANK))


def far_product(left, right):
    l1, l2, l3 = terms(left)
    r1, r2, r3 = terms(right)
    return dot(jnp.concatenate([l1, l1, l2, l1, l3, l2], axis=1), jnp.concatenate([r1, r2, r1, r3, r1, r2], axis=0))


def invert_factor(tiles, write):
    lane = lax.broadcasted_iota(jnp.int32, (SUB, RANK), 1)
    sub = lax.broadcasted_iota(jnp.int32, (SUB, RANK), 0)
    count = len(tiles)
    for b in range(count):
        first = b * SUB
        panel = (lane >= first) & (lane < first + SUB)
        near, far = range(b, min(b + 3, count)), range(b + 3, count)
        columns = {
            t: [jnp.broadcast_to(tiles[t][:, first + k:first + k + 1], (SUB, RANK)) for k in range(SUB)] for t in near
        }
        pivot = [[spread(columns[b][j][k:k + 1]) if k >= j else None for k in range(SUB)] for j in range(SUB)]
        rows = [jnp.where(panel, (lane == first + p).astype(jnp.float32), spread(tiles[b][p:p + 1])) for p in range(SUB)]
        inverse = []
        for j in range(SUB):
            inverse.append(1.0 / pivot[j][j])
            for i in range(j + 1, SUB):
                ratio = pivot[j][i] * inverse[j]
                for k in range(i, SUB):
                    pivot[i][k] = pivot[i][k] - ratio * pivot[j][k]
                rows[i] = rows[i] - ratio * rows[j]
        for t in near[1:]:
            held = jnp.where(panel, 0.0, tiles[t])
            left = columns[t]
            for j in range(SUB):
                multiple = left[j] * inverse[j]
                for k in range(j + 1, SUB):
                    left[k] = left[k] - multiple * pivot[j][k]
                held = held - multiple * rows[j]
            tiles[t] = held
        if far:
            back = [None] * SUB
            for j in reversed(range(SUB)):
                row = rows[j]
                for k in range(j + 1, SUB):
                    row = row - pivot[j][k] * back[k]
                back[j] = row * inverse[j]
            block = back[0]
            for p in range(1, SUB):
                block = jnp.where(sub == p, back[p], block)
            zero = jnp.zeros((SUB, RANK), jnp.float32)
            block = jnp.concatenate([zero] * b + [block] + [zero] * (count - 1 - b), axis=0)
            taken = far_product(jnp.concatenate([tiles[t] for t in far], axis=0), block)
            for place, t in enumerate(far):
                tiles[t] = jnp.where(panel, 0.0, tiles[t]) - taken[place * SUB:(place + 1) * SUB]
        for p in range(SUB):
            d = pivot[p][p]
            root = lax.rsqrt(d)
            root = root * (1.5 - 0.5 * d * root * root)
            write(first + p, jnp.where(lane <= first + p, rows[p] * root, 0.0)[0:1])


def whiten_kernel(whole_ref, inverse_ref, reduced_ref, squares_ref):
    count, high, _ = whole_ref.shape
    share = RANK // count
    own = high - share
    tiles = [whole_ref[k, t:t + SUB] for k in range(count) for t in range(own, high, SUB)]

    def write(row, value):
        inverse_ref[row:row + 1, :] = value

    invert_factor(tiles, write)
    right_raw = jnp.concatenate([whole_ref[k, :own] for k in range(count)], axis=0)
    reduced = outer_cols(right_raw, inverse_ref[...]) * (1.0 / REPLICAS)
    reduced_ref[...] = reduced
    squares = jnp.sum(reduced * reduced, axis=0, keepdims=True)
    for k in range(squares_ref.shape[0]):
        squares_ref[k] = squares


def whiten_right(whole, n_tensor):
    count, high, _ = whole.shape
    cols = count * high - RANK
    vmem = pl.BlockSpec(memory_space=pltpu.VMEM)
    return pl.pallas_call(
        whiten_kernel,
        out_shape=(
            jax.ShapeDtypeStruct((RANK, RANK), jnp.float32),
            jax.ShapeDtypeStruct((cols, RANK), jnp.float32),
            jax.ShapeDtypeStruct((n_tensor, 1, RANK), jnp.float32),
        ),
        in_specs=[vmem],
        out_specs=[vmem] * 3,
        compiler_params=pltpu.CompilerParams(vmem_limit_bytes=16 * 2**20),
    )(whole)


def project_kernel(blended_ref, right_ref, out_ref):
    out_ref[...] = six_products(terms(blended_ref[...]), terms(right_ref[...]))


def project(blended, right):
    vmem = pl.BlockSpec(memory_space=pltpu.VMEM)
    return pl.pallas_call(
        project_kernel,
        out_shape=jax.ShapeDtypeStruct((blended.shape[0], RANK), jnp.float32),
        in_specs=[vmem] * 2,
        out_specs=vmem,
        compiler_params=pltpu.CompilerParams(vmem_limit_bytes=24 * 2**20),
    )(blended, right)


def resum_kernel(high, parts_ref, out_ref):
    slab = high * SUB
    starts = range(0, parts_ref.shape[0], slab)
    total = sum(parts_ref[start:start + slab, :] for start in starts)
    block = sum(total[k * high:(k + 1) * high] for k in range(SUB))
    copies = jnp.concatenate([block] * SUB, axis=0)
    for start in starts:
        out_ref[start:start + slab, :] = copies


def resum(parts, count):
    vmem = pl.BlockSpec(memory_space=pltpu.VMEM)
    return pl.pallas_call(
        functools.partial(resum_kernel, parts.shape[0] // count),
        out_shape=jax.ShapeDtypeStruct(parts.shape, jnp.float32),
        in_specs=[vmem],
        out_specs=vmem,
        compiler_params=pltpu.CompilerParams(vmem_limit_bytes=16 * 2**20),
    )(parts)


def inner_kernel(blended_ref, projected_ref, out_ref):
    count, share = out_ref.shape[0], RANK // out_ref.shape[0]
    own = out_ref.shape[1] - share
    cols = count * own
    projected = projected_ref[...]
    both = six_products(terms(jnp.concatenate([blended_ref[...], projected], axis=1).T), terms(projected))
    for k in range(count):
        out_ref[k, :own] = both[k * own:(k + 1) * own]
        out_ref[k, own:] = both[cols + k * share:cols + (k + 1) * share]


def inner_products(blended, projected, count):
    rows, cols = blended.shape
    vmem = pl.BlockSpec(memory_space=pltpu.VMEM)
    return pl.pallas_call(
        inner_kernel,
        out_shape=jax.ShapeDtypeStruct((count, (cols + RANK) // count, RANK), jnp.float32),
        in_specs=[vmem] * 2,
        out_specs=vmem,
        compiler_params=pltpu.CompilerParams(vmem_limit_bytes=24 * 2**20),
    )(blended, projected)


def halves(x):
    high = x.astype(jnp.bfloat16)
    return high, (x - high.astype(jnp.float32)).astype(jnp.bfloat16)


def outer_of_halves(left, right):
    def outer(left, right):
        return lax.dot_general(left, right, (((1,), (1,)), ((), ())), preferred_element_type=jnp.float32)

    return outer(left[0], right[0]) + (outer(left[0], right[1]) + outer(left[1], right[0]))


def moment_kernel(blended_ref, projected_ref, inverse_ref, reduced_ref, left_ref, moment_out, moment_ref, sems):
    steps = sems.shape[0]
    rows = left_ref.shape[0] // steps
    inverse = inverse_ref[...]
    right = halves(reduced_ref[...] * (1.0 - decay_rate))
    copies = []
    for step in range(steps):
        block = pl.ds(step * rows, rows)
        left = outer_cols(projected_ref[block, :], inverse)
        left_ref[block, :] = left
        moment_ref[block, :] = blended_ref[block, :] - outer_of_halves(halves(left), right)
        copies.append(pltpu.make_async_copy(moment_ref.at[block], moment_out.at[block], sems.at[step]))
        copies[-1].start()
    for copy in copies:
        copy.wait()


def left_and_moment(blended, projected, inverse_low, reduced):
    steps = 4
    rows, cols = blended.shape
    vmem, anywhere = pl.BlockSpec(memory_space=pltpu.VMEM), pl.BlockSpec(memory_space=pl.ANY)
    return pl.pallas_call(
        moment_kernel,
        out_shape=(
            jax.ShapeDtypeStruct((rows, RANK), jnp.float32),
            jax.ShapeDtypeStruct((rows, cols), jnp.float32),
        ),
        in_specs=[vmem] * 4,
        out_specs=[vmem, anywhere],
        scratch_shapes=[pltpu.VMEM((rows, cols), jnp.float32), pltpu.SemaphoreType.DMA((steps,))],
        compiler_params=pltpu.CompilerParams(vmem_limit_bytes=24 * 2**20),
        cost_estimate=pl.CostEstimate(
            flops=12 * rows * cols * RANK, bytes_accessed=4 * rows * cols, transcendentals=0
        ),
    )(blended, projected, inverse_low, reduced)


def update_kernel(left_ref, reduced_ref, squares_ref, right_out, update_out, right_ref, update_ref, sems):
    steps = sems.shape[0] - 1
    rows = left_ref.shape[0] // steps

    norm = jnp.sqrt(jnp.sum(squares_ref[...], axis=0)) + epsilon
    right_new = reduced_ref[...] / norm
    right_ref[...] = right_new
    copies = [pltpu.make_async_copy(right_ref, right_out, sems.at[steps])]
    copies[0].start()
    right = halves(right_new * math.sqrt(M_ROWS * N_COLS / RANK))
    for step in range(steps):
        block = pl.ds(step * rows, rows)
        update_ref[block, :] = outer_of_halves(halves(left_ref[block, :]), right).astype(jnp.bfloat16)
        copies.append(pltpu.make_async_copy(update_ref.at[block], update_out.at[block], sems.at[step]))
        copies[-1].start()
    for copy in copies:
        copy.wait()


def update_and_right(left, reduced, squares):
    steps = 4
    rows, cols = left.shape[0], reduced.shape[0]
    vmem, anywhere = pl.BlockSpec(memory_space=pltpu.VMEM), pl.BlockSpec(memory_space=pl.ANY)
    return pl.pallas_call(
        update_kernel,
        out_shape=(
            jax.ShapeDtypeStruct((cols, RANK), jnp.float32),
            jax.ShapeDtypeStruct((rows, cols), jnp.bfloat16),
        ),
        in_specs=[vmem] * 3,
        out_specs=[anywhere] * 2,
        scratch_shapes=[
            pltpu.VMEM((cols, RANK), jnp.float32),
            pltpu.VMEM((rows, cols), jnp.bfloat16),
            pltpu.SemaphoreType.DMA((steps + 1,)),
        ],
        compiler_params=pltpu.CompilerParams(vmem_limit_bytes=16 * 2**20),
    )(left, reduced, squares)


def scatter_sum(blocks, axes):
    return jnp.sum(lax.all_to_all(blocks, axes, 0, 0), axis=0)


def gather(block, axes, count):
    return lax.all_to_all(jnp.broadcast_to(block, (count,) + block.shape), axes, 0, 0)


def body(momentum, gradient, right_factor):
    n_far, n_near, n_fsdp, n_tensor = (lax.axis_size(a) for a in ("dp_far", "dp_near", "fsdp", "tensor"))
    blended = momentum[0, 0] + gradient[0, 0].astype(jnp.float32)
    rows, cols = blended.shape
    plane = ("dp_far", "dp_near", "tensor")
    count = n_far * n_near * n_tensor
    lines = (count, 1, rows // count * RANK)
    partial = lax.optimization_barrier(project(blended, right_factor[0]))
    parts = lax.all_to_all(partial.reshape(lines), plane, 0, 0).reshape(rows, RANK)
    copies = resum(parts, count)
    projected = lax.all_to_all(copies.reshape(lines), plane, 0, 0).reshape(rows, RANK)
    group = ("fsdp", "dp_near")
    count = n_fsdp * n_near
    own = cols // count
    held = scatter_sum(inner_products(blended, projected, count), group)
    right_raw, gram = lax.optimization_barrier((held[:own], held[own:] * (1.0 / n_near)))
    summed, gram = lax.optimization_barrier((jnp.sum(gather(right_raw, "dp_far", n_far), axis=0), gram))
    whole = gather(jnp.concatenate([summed, gram], axis=0), group, count)
    inverse_low, reduced, squares = whiten_right(whole, n_tensor)
    squares = lax.all_to_all(squares, "tensor", 0, 0)
    orthonormal, moment = left_and_moment(blended, projected, inverse_low, reduced)
    right_new, update = update_and_right(orthonormal, reduced, squares)
    return moment[None, None], right_new[None], update[None]


def solution(mesh):
    near = 2
    n_dp, n_fsdp, n_tensor = (mesh.shape[a] for a in ("dp", "fsdp", "tensor"))
    devices = mesh.devices.reshape(n_dp // near, near, n_fsdp, n_tensor)
    mesh = jax.sharding.Mesh(devices, ("dp_far", "dp_near", "fsdp", "tensor"))
    dp = ("dp_far", "dp_near")
    in_specs = (
        P(dp, None, "fsdp", "tensor"),
        P(dp, None, "fsdp", "tensor"),
        P(None, "tensor", None),
    )
    out_specs = (
        P(dp, None, "fsdp", "tensor"),
        P(None, "tensor", None),
        P(None, "fsdp", "tensor"),
    )
    return jax.shard_map(body, mesh=mesh, in_specs=in_specs, out_specs=out_specs, check_vma=False)
```
